128 devices in a mesh: fsdp: 16 (over y, x), tp: 8 (over z, core).
Axes of the slice: x: 4, y: 4, z: 4, core: 2. Of those that a mesh axis runs over, the one named last changes fastest.
Arguments:
- momentum_square: float32 [2, 8192, 8192], P(None, 'fsdp', 'tp'), may hold values from -6 to 6
- grad_square: bfloat16 [2, 8192, 8192], P(None, 'fsdp', 'tp'), may hold values from -6 to 6
- basis_square: float32 [2, 8192, 256], P(None, 'tp'), may hold values from -0.0625 to 0.0625
- momentum_narrow: float32 [2, 8192, 1024], P(None, 'fsdp', 'tp'), may hold values from -6 to 6
- grad_narrow: bfloat16 [2, 8192, 1024], P(None, 'fsdp', 'tp'), may hold values from -6 to 6
- basis_narrow: float32 [2, 1024, 256], P(None, 'tp'), may hold values from -0.1875 to 0.1875
Outputs:
- new_momentum_square: float32 [2, 8192, 8192], P(None, 'fsdp', 'tp')
- new_basis_square: float32 [2, 8192, 256], P(None, 'tp')
- update_square: bfloat16 [2, 8192, 8192], P(None, 'fsdp', 'tp')
- new_momentum_narrow: float32 [2, 8192, 1024], P(None, 'fsdp', 'tp')
- new_basis_narrow: float32 [2, 1024, 256], P(None, 'tp')
- update_narrow: bfloat16 [2, 8192, 1024], P(None, 'fsdp', 'tp')
The draws below stay inside these ranges and needn't reach their ends.
All inputs are finite; a program needn't handle non-finite values.
Results may differ from the reference program's by a relative error of at most 0.0015.
Values sent between devices are 32-bit elements; how exact they have to be, the bound alone decides.
A program may use at most 128 MiB of HBM per device.

```python
import math
import jax
import jax.numpy as jnp
from jax import lax

D = 8192
KVW = 1024
RANK = 256


def steps_of(stream_key, extent, cuts, least, largest):
    def one(axis_at, blocks):
        steps = jax.random.uniform(jax.random.fold_in(jax.random.fold_in(stream_key, 6), axis_at), (blocks,), jnp.float32, least / len(cuts), largest / len(cuts))
        return jnp.repeat(jnp.exp(steps), extent[axis_at] // blocks).reshape((-1,) + (1,) * (len(extent) - axis_at - 1))

    factor_of = one(*cuts[0])
    for cut in cuts[1:]:
        factor_of = factor_of * one(*cut)
    return factor_of


def bell_draw(own_key, extent, scale, reach, split=(), kind=jnp.bfloat16):
    array = jax.random.normal(own_key, extent, jnp.float32) * scale
    if len(split) > 0:
        array = steps_of(own_key, extent, split, -0.22, 0.18) * array
    return jnp.clip(array, min=-reach, max=reach).astype(kind)


def setup_inputs(seed: int = 0) -> dict:
    keys = jax.random.split(jax.random.key(seed), 7)
    return {
        "momentum_square": bell_draw(keys[0], (2, D, D), 1.0, 6.0, ((1, 16), (2, 8)), jnp.float32),
        "grad_square": bell_draw(keys[1], (2, D, D), 1.0, 6.0, ((1, 16), (2, 8))),
        "basis_square": bell_draw(keys[2], (2, D, RANK), D ** -0.5, 0.0625, ((1, 8),), jnp.float32),
        "momentum_narrow": bell_draw(keys[3], (2, D, KVW), 1.0, 6.0, ((1, 16), (2, 8)), jnp.float32),
        "grad_narrow": bell_draw(keys[4], (2, D, KVW), 1.0, 6.0, ((1, 16), (2, 8))),
        "basis_narrow": bell_draw(keys[5], (2, KVW, RANK), KVW ** -0.5, 0.1875, ((1, 8),), jnp.float32),
    }


MOMENTUM = 0.9

def dion_group(momentum, grad, basis):
    highest = lax.Precision.HIGHEST
    buffer = momentum + grad.astype(jnp.float32)
    projected = jnp.einsum('kmn,knr->kmr', buffer, basis, precision=highest)
    gram_matrix = jnp.einsum('kmr,kms->krs', projected, projected, precision=highest)
    factor_lower = jnp.linalg.cholesky(gram_matrix)
    solved = jax.scipy.linalg.solve_triangular(factor_lower, jnp.swapaxes(projected, 1, 2), lower=True)
    left = jnp.swapaxes(solved, 1, 2)
    back = jnp.einsum('kmn,kmr->knr', buffer, left, precision=highest)
    new_momentum = buffer - (1.0 - MOMENTUM) * jnp.einsum('kmr,knr->kmn', left, back, precision=highest)
    squares = lax.optimization_barrier(jnp.sum(back * back, axis=1))
    new_basis = back / (jnp.sqrt(squares) + 1e-06)[:, None, :]
    scaling = math.sqrt(buffer.shape[1] * buffer.shape[2] / RANK)
    update = (scaling * jnp.einsum('kmr,knr->kmn', left, new_basis, precision=highest)).astype(jnp.bfloat16)
    return (new_momentum, new_basis, update)

def reference(momentum_square, grad_square, basis_square, momentum_narrow, grad_narrow, basis_narrow):
    mom_square, new_basis_sq, update_sq = dion_group(momentum_square, grad_square, basis_square)
    mom_narrow, new_basis_nw, update_nw = dion_group(momentum_narrow, grad_narrow, basis_narrow)
    return (mom_square, new_basis_sq, update_sq, mom_narrow, new_basis_nw, update_nw)
```

```python
import math

import jax
import jax.numpy as jnp
from jax import lax
from jax.experimental import pallas as pl
from jax.experimental.pallas import tpu as pltpu
from jax.sharding import PartitionSpec as P

RANK = 256
MOMENTUM = 0.9
MESH = pl.DeviceIdType.MESH
F32 = jnp.float32
BF16 = jnp.bfloat16
PANEL = 32
GROUP = 8
VMEM_LIMIT = 56 * 2**20

RING_X, RING_Y, RING_Z = 4, 4, 4


def split(x):
    hi = x.astype(BF16)
    return hi, (x - hi.astype(F32)).astype(BF16)


def mm(a, b, dims=((1,), (0,))):
    return lax.dot_general(a, b, (dims, ((), ())), preferred_element_type=F32)


def dot3(a, b, dims=((1,), (0,))):
    return mm(a[0], b[0], dims) + (mm(a[0], b[1], dims) + mm(a[1], b[0], dims))


def dot6(a, b, dims=((1,), (0,))):
    return lax.dot_general(
        a, b, (dims, ((), ())), precision=lax.Precision.HIGHEST, preferred_element_type=F32
    )


class Links:
    def __init__(self, send, recv):
        self.send, self.recv, self.used = send, recv, 0

    def take(self, count):
        self.used += count
        return self.used - count

    def copy(self, index, src, dst, device):
        return pltpu.make_async_remote_copy(
            src_ref=src,
            dst_ref=dst,
            send_sem=self.send.at[index],
            recv_sem=self.recv.at[index],
            device_id=device,
            device_id_type=MESH,
        )


class Scatter:
    def __init__(self, links, me, right, left, part, half, inbox):
        self.me, self.part, self.half, self.inbox = me, part, half, inbox
        self.after, self.before = lax.rem(me + 1, 4), lax.rem(me + 3, 4)
        opposite = lax.rem(me + 2, 4)
        base = links.take(6)

        def outgoing(slot, view, device):
            return links.copy(base + slot, view, inbox.at[slot], device)

        h = half
        self.r1 = outgoing(0, part(opposite, 0, h), right)
        self.r2 = outgoing(1, part(self.after, h, h), right)
        self.r3 = outgoing(2, part(self.after, 0, h), right)
        self.l1 = outgoing(3, part(opposite, h, h), left)
        self.l2 = outgoing(4, part(self.before, 0, h), left)
        self.l3 = outgoing(5, part(self.before, h, h), left)

    def start(self):
        for c in (self.r1, self.l1, self.r2, self.l2):
            c.start()

    def middle(self):
        h = self.half
        self.r1.wait_recv()
        view = self.part(self.after, 0, h)
        view[...] = view[...] + self.inbox[0]
        self.r3.start()
        self.l1.wait_recv()
        view = self.part(self.before, h, h)
        view[...] = view[...] + self.inbox[3]
        self.l3.start()

    def end(self, target):
        h = self.half
        self.r2.wait_recv()
        self.l2.wait_recv()
        self.r3.wait_recv()
        target(0, h)[...] = self.part(self.me, 0, h)[...] + (self.inbox[2] + self.inbox[4])
        self.l3.wait_recv()
        target(h, h)[...] = self.part(self.me, h, h)[...] + (self.inbox[1] + self.inbox[5])

    def drain(self):
        for c in (self.r1, self.r2, self.r3, self.l1, self.l2, self.l3):
            c.wait_send()


class Gather:
    def __init__(self, links, me, right, left, part, half):
        after, before = lax.rem(me + 1, 4), lax.rem(me + 3, 4)
        base = links.take(4)
        h = half

        def outgoing(slot, view, device):
            return links.copy(base + slot, view, view, device)

        self.r1 = outgoing(0, part(me, 0, 2 * h), right)
        self.l1 = outgoing(1, part(me, 0, 2 * h), left)
        self.r2 = outgoing(2, part(before, 0, h), right)
        self.l2 = outgoing(3, part(after, h, h), left)

    def start(self):
        self.r1.start()
        self.l1.start()

    def middle(self):
        self.r1.wait_recv()
        self.r2.start()
        self.l1.wait_recv()
        self.l2.start()

    def end(self):
        self.r2.wait_recv()
        self.l2.wait_recv()

    def drain(self):
        for c in (self.r1, self.l1, self.r2, self.l2):
            c.wait_send()


def factor_block(a):
    rows = lax.broadcasted_iota(jnp.int32, (PANEL, 128), 0)
    done = []
    for s in range(0, PANEL, GROUP):
        n = PANEL - s
        cols = [jnp.broadcast_to(a[s:, s + j : s + j + 1], (n, 128)) for j in range(GROUP)]
        lines = [a[s + j : s + j + 1, :] for j in range(GROUP)]
        rest = a[s + GROUP :]
        for j in range(GROUP):
            pivot = cols[j][j : j + 1, :]
            m = jnp.where(rows[s:] > s + j, cols[j] * (1.0 / pivot), 0.0)
            for q in range(j + 1, GROUP):
                cols[q] = cols[q] - m * cols[q][j : j + 1, :]
            for q in range(j + 1, GROUP):
                lines[q] = lines[q] - m[q : q + 1, :] * lines[j]
            if n > GROUP:
                rest = rest - m[GROUP:] * lines[j]
            done.append(lines[j] * lax.rsqrt(pivot))
        if n > GROUP:
            a = jnp.concatenate([a[: s + GROUP], rest], axis=0)
    return jnp.concatenate(done, axis=0)


def cholesky_start(gram, work):
    n = RANK
    work[:, :n] = gram[...]
    eye = lax.broadcasted_iota(jnp.int32, (n, n), 0) == lax.broadcasted_iota(jnp.int32, (n, n), 1)
    work[:, n:] = eye.astype(F32)


def cholesky_panels(work, inverse, first, last):
    n = RANK
    lane = lax.broadcasted_iota(jnp.int32, (PANEL, 128), 1)
    row = lax.broadcasted_iota(jnp.int32, (PANEL, 128), 0)

    def panel(k, carry):
        off = pl.multiple_of(k * PANEL, PANEL)
        band = work[pl.ds(off, PANEL), :]
        block = pltpu.roll(band[:, :n], lax.rem(n - off, n), axis=1)[:, :128]
        both = jnp.where(lane < PANEL, block, jnp.where(lane == row + PANEL, 1.0, 0.0))
        block_inverse = factor_block(both)[:, PANEL : 2 * PANEL]
        band = dot6(block_inverse, band)
        inverse[pl.ds(off, PANEL), :] = band[:, n:]
        work[...] = work[...] - dot6(band[:, :n], band, ((0,), (0,)))
        return carry

    lax.fori_loop(first, last, panel, 0)


def orthonormal_kernel(
    mom_sq, grad_sq, basis_sq, mom_nw, grad_nw, basis_nw,
    left_out, back_out, squares_out,
    mom_sq_v, grad_sq_v, basis_sq_v, mom_nw_v, grad_nw_v, basis_nw_v,
    buf_sq_hi, buf_sq_lo, buf_nw_hi, buf_nw_lo,
    partial, held, projected, scatter_z,
    gram_part, gram_in, gram, chol_work, inverse,
    sums, wide, scatter_1, scatter_2,
    norms,
    load_sem, send_sem, recv_sem, gram_send, gram_recv, gram_send2, gram_recv2, norm_send, norm_recv,
):
    f, t = lax.axis_index("fsdp"), lax.axis_index("tp")
    y, x = f // RING_X, lax.rem(f, RING_X)
    z, core = t // 2, lax.rem(t, 2)
    other = 1 - core
    fsdp_count = RING_X * RING_Y
    tp_count = RING_Z * 2
    links = Links(send_sem, recv_sem)

    def at(y=y, x=x, z=z, core=core):
        return (y * RING_X + x, z * 2 + core)

    def step(value, by):
        return lax.rem(value + by, 4)

    sibling = at(core=other)
    x_right, x_left = at(x=step(x, 1)), at(x=step(x, 3))
    y_right, y_left = at(y=step(y, 1)), at(y=step(y, 3))
    z_right, z_left = at(z=step(z, 1)), at(z=step(z, 3))

    barrier = pltpu.get_barrier_semaphore()

    def greet_fsdp(k, carry):
        peer = lax.rem(f + k, fsdp_count)
        pl.semaphore_signal(barrier, inc=1, device_id=(peer, t), device_id_type=MESH)
        return carry

    def greet_tp(k, carry):
        peer = lax.rem(t + k, tp_count)
        pl.semaphore_signal(barrier, inc=1, device_id=(f, peer), device_id_type=MESH)
        return carry

    lax.fori_loop(1, fsdp_count, greet_fsdp, 0)
    lax.fori_loop(1, tp_count, greet_tp, 0)

    loads = []
    for k in range(2):
        for n, (src, dst) in enumerate(
            ((basis_sq, basis_sq_v), (mom_sq, mom_sq_v), (grad_sq, grad_sq_v))
        ):
            loads.append(pltpu.make_async_copy(src.at[k], dst.at[k], load_sem.at[k * 3 + n]))
    for n, (src, dst) in enumerate(
        ((basis_nw, basis_nw_v), (mom_nw, mom_nw_v), (grad_nw, grad_nw_v))
    ):
        loads.append(pltpu.make_async_copy(src, dst, load_sem.at[6 + n]))
    for c in loads:
        c.start()

    def rows_of(which):
        return pl.ds(pl.multiple_of(which * 256, 256), 256)

    core_base = links.take(4)
    core_copies = [
        links.copy(core_base + i, partial.at[i, rows_of(other)], held.at[i], sibling)
        for i in range(4)
    ]

    def project(i, mom, grad, basis, hi, lo):
        pair = split(basis[...])
        for place, which in enumerate((other, core)):
            rows = rows_of(which)
            b_hi, b_lo = split(mom[rows, :] + grad[rows, :].astype(F32))
            hi[rows, :] = b_hi
            lo[rows, :] = b_lo
            partial[i, rows, :] = dot3((b_hi, b_lo), pair)
            if place == 0:
                if i == 0:
                    pl.semaphore_wait(barrier, fsdp_count + tp_count - 2)
                core_copies[i].start()

    for k in range(2):
        for c in loads[k * 3 : k * 3 + 3]:
            c.wait()
        project(
            k, mom_sq_v.at[k], grad_sq_v.at[k], basis_sq_v.at[k], buf_sq_hi.at[k], buf_sq_lo.at[k]
        )
    for c in loads[6:]:
        c.wait()
    for k in range(2):
        project(
            2 + k, mom_nw_v.at[k], grad_nw_v.at[k], basis_nw_v.at[k], buf_nw_hi.at[k], buf_nw_lo.at[k]
        )
    for i in range(4):
        core_copies[i].wait_recv()
        held[i] = held[i] + partial[i, rows_of(core), :]

    z_sum = Scatter(
        links, z, z_right, z_left, lambda i, a, n: held.at[i, pl.ds(a, n)], 128, scatter_z
    )

    def own_rows(i, a, n):
        return projected.at[i, pl.ds(pl.multiple_of(core * 256 + a, 128), n)]

    z_all = Gather(links, z, z_right, z_left, own_rows, 128)
    z_sum.start()
    z_sum.middle()
    z_sum.end(lambda a, n: own_rows(z, a, n))
    z_all.start()

    core_base = links.take(4)

    def core_send(n, i):
        view = own_rows(i, 0, 256)
        return links.copy(core_base + n, view, view, sibling)

    across = [core_send(n, step(z, by)) for n, by in enumerate((0, 3, 1, 2))]
    across[0].start()

    across[0].wait_recv()
    gram_cols = pl.ds(pl.multiple_of(core * 128, 128), 128)
    gram_part[...] = dot6(projected[z, :, gram_cols], projected[z], ((0,), (0,)))

    def gram_rows(i):
        return pl.ds(pl.multiple_of(i * 8, 8), 8)

    def gram_copy(peer, slot):
        return pltpu.make_async_remote_copy(
            src_ref=gram_part.at[gram_rows(peer)],
            dst_ref=gram_in.at[slot],
            send_sem=gram_send.at[peer],
            recv_sem=gram_recv.at[slot],
            device_id=(peer, t),
            device_id_type=MESH,
        )

    def gram_out(k, carry):
        gram_copy(lax.rem(f + k, fsdp_count), f).start()
        return carry

    lax.fori_loop(1, fsdp_count, gram_out, 0)
    gram_in[f] = gram_part[gram_rows(f), :]

    z_all.middle()
    across[1].start()
    across[2].start()

    def gram_arrive(k, carry):
        gram_copy(lax.rem(f + k, fsdp_count), lax.rem(f + k, fsdp_count)).wait_recv()
        return carry

    lax.fori_loop(1, fsdp_count, gram_arrive, 0)

    def full_rows(i):
        return pl.ds(pl.multiple_of(core * 128 + i * 8, 8), 8)

    gram[full_rows(f), :] = jnp.sum(gram_in[...], axis=0)

    def gram_copy2(peer, slot):
        view = gram.at[full_rows(slot)]
        return pltpu.make_async_remote_copy(
            src_ref=view,
            dst_ref=view,
            send_sem=gram_send2.at[peer],
            recv_sem=gram_recv2.at[slot],
            device_id=(peer, t),
            device_id_type=MESH,
        )

    def gram_out2(k, carry):
        gram_copy2(lax.rem(f + k, fsdp_count), f).start()
        return carry

    lax.fori_loop(1, fsdp_count, gram_out2, 0)

    z_all.end()
    across[3].start()
    for c in across[1:]:
        c.wait_recv()

    def back_product(k):
        sq = split(projected[k].T)
        sums[k, :, :1024] = dot3(sq, (buf_sq_hi[k], buf_sq_lo[k]))
        nw = split(projected[2 + k].T)
        sums[k, :, 1024:] = dot3(nw, (buf_nw_hi[k], buf_nw_lo[k]))

    def wide_rows(ref, k):
        return lambda i, a, n: ref.at[k, pl.ds(pl.multiple_of(i * 64 + a, 8), n)]

    def narrow_rows(ref, k, outer):
        return lambda i, a, n: ref.at[k, pl.ds(pl.multiple_of(outer * 64 + i * 16 + a, 8), n)]

    sum_1 = [
        Scatter(links, x, x_right, x_left, wide_rows(sums, 0), 32, scatter_1.at[0]),
        Scatter(links, y, y_right, y_left, wide_rows(sums, 1), 32, scatter_1.at[1]),
    ]
    sum_2 = [
        Scatter(links, y, y_right, y_left, narrow_rows(sums, 0, x), 8, scatter_2.at[0]),
        Scatter(links, x, x_right, x_left, narrow_rows(sums, 1, y), 8, scatter_2.at[1]),
    ]
    all_1 = [
        Gather(links, y, y_right, y_left, narrow_rows(wide, 0, x), 8),
        Gather(links, x, x_right, x_left, narrow_rows(wide, 1, y), 8),
    ]
    all_2 = [
        Gather(links, x, x_right, x_left, wide_rows(wide, 0), 32),
        Gather(links, y, y_right, y_left, wide_rows(wide, 1), 32),
    ]
    outer, inner = (x, y), (y, x)

    back_product(0)
    sum_1[0].start()
    back_product(1)
    sum_1[1].start()

    def gram_arrive2(k, carry):
        gram_copy2(lax.rem(f + k, fsdp_count), lax.rem(f + k, fsdp_count)).wait_recv()
        return carry

    lax.fori_loop(1, fsdp_count, gram_arrive2, 0)
    half_rows = gram.at[pl.ds(pl.multiple_of(core * 128, 128), 128)]
    gram_across = links.copy(links.take(1), half_rows, half_rows, sibling)
    gram_across.start()
    gram_across.wait_recv()

    own_inverse = inverse.at[z]
    cholesky_start(gram, chol_work)
    cholesky_panels(chol_work, own_inverse, 0, 1)
    for k in range(2):
        sum_1[k].middle()
    cholesky_panels(chol_work, own_inverse, 1, 3)
    for k in range(2):
        sum_1[k].end(lambda a, n, k=k: wide_rows(sums, k)(outer[k], a, n))
        sum_2[k].start()
    cholesky_panels(chol_work, own_inverse, 3, 4)
    for k in range(2):
        sum_2[k].middle()
    cholesky_panels(chol_work, own_inverse, 4, 5)
    for k in range(2):
        sum_2[k].end(lambda a, n, k=k: narrow_rows(wide, k, outer[k])(inner[k], a, n))
        all_1[k].start()
    cholesky_panels(chol_work, own_inverse, 5, 6)
    for k in range(2):
        all_1[k].middle()
    cholesky_panels(chol_work, own_inverse, 6, 7)
    for k in range(2):
        all_1[k].end()
        all_2[k].start()
    cholesky_panels(chol_work, own_inverse, 7, 8)

    def inverse_rows(i, a, n):
        return inverse.at[i, pl.ds(pl.multiple_of(core * 128 + a, 64), n)]

    inv_all = Gather(links, z, z_right, z_left, inverse_rows, 64)
    inv_all.start()
    core_base = links.take(3)

    def inverse_send(n, i):
        view = inverse_rows(i, 0, 128)
        return links.copy(core_base + n, view, view, sibling)

    inv_across = [inverse_send(n, step(z, by)) for n, by in enumerate((3, 1, 2))]
    inv_all.middle()
    inv_across[0].start()
    inv_across[1].start()
    for k in range(2):
        all_2[k].middle()
    inv_all.end()
    inv_across[2].start()
    for c in inv_across:
        c.wait_recv()

    for i in range(4):
        left_out[i] = dot3(split(projected[i]), split(inverse[i]), ((1,), (1,)))

    norms[t] = jnp.zeros((8, RANK), F32)
    for k in range(2):
        all_2[k].end()
        for i, cols in ((k, slice(0, 1024)), (2 + k, slice(1024, 1152))):
            back = dot3(split(inverse[i]), split(wide[k, :, cols]))
            back_out[k, :, cols] = back
            square = dot6(jnp.ones((8, back.shape[1]), F32), back * back, ((1,), (1,)))
            norms[t, pl.ds(i, 1), :] = square[:1]

    def norm_copy(peer, slot):
        return pltpu.make_async_remote_copy(
            src_ref=norms.at[t],
            dst_ref=norms.at[slot],
            send_sem=norm_send.at[peer],
            recv_sem=norm_recv.at[slot],
            device_id=(f, peer),
            device_id_type=MESH,
        )

    def norm_out(k, carry):
        norm_copy(lax.rem(t + k, tp_count), t).start()
        return carry

    def norm_arrive(k, carry):
        norm_copy(lax.rem(t + k, tp_count), lax.rem(t + k, tp_count)).wait_recv()
        return carry

    lax.fori_loop(1, tp_count, norm_out, 0)
    lax.fori_loop(1, tp_count, norm_arrive, 0)
    squares_out[...] = jnp.sum(norms[...], axis=0)

    for c in core_copies + across + inv_across + [gram_across]:
        c.wait_send()
    for ring in [z_sum, z_all, inv_all] + sum_1 + sum_2 + all_1 + all_2:
        ring.drain()

    def gram_drain(k, carry):
        peer = lax.rem(f + k, fsdp_count)
        gram_copy(peer, f).wait_send()
        gram_copy2(peer, f).wait_send()
        return carry

    def norm_drain(k, carry):
        norm_copy(lax.rem(t + k, tp_count), t).wait_send()
        return carry

    lax.fori_loop(1, fsdp_count, gram_drain, 0)
    lax.fori_loop(1, tp_count, norm_drain, 0)


def orthonormal(mom_sq, grad_sq, basis_sq, mom_nw, grad_nw, basis_nw):
    rows = mom_sq.shape[1]
    wide, thin = mom_sq.shape[2], mom_nw.shape[2]
    both = wide + thin
    vmem = pltpu.VMEM
    dma = pltpu.SemaphoreType.DMA
    whole = pl.BlockSpec(memory_space=pltpu.VMEM)
    return pl.pallas_call(
        orthonormal_kernel,
        out_shape=(
            jax.ShapeDtypeStruct((4, rows, RANK), F32),
            jax.ShapeDtypeStruct((2, RANK, both), F32),
            jax.ShapeDtypeStruct((8, RANK), F32),
        ),
        in_specs=[pl.BlockSpec(memory_space=pl.ANY)] * 6,
        out_specs=(whole, whole, whole),
        scratch_shapes=[
            vmem(mom_sq.shape, F32),
            vmem(grad_sq.shape, BF16),
            vmem(basis_sq.shape, F32),
            vmem(mom_nw.shape, F32),
            vmem(grad_nw.shape, BF16),
            vmem(basis_nw.shape, F32),
            vmem(mom_sq.shape, BF16),
            vmem(mom_sq.shape, BF16),
            vmem(mom_nw.shape, BF16),
            vmem(mom_nw.shape, BF16),
            vmem((4, rows, RANK), F32),
            vmem((4, rows // 2, RANK), F32),
            vmem((4, rows, RANK), F32),
            vmem((6, rows // 4, RANK), F32),
            vmem((128, RANK), F32),
            vmem((16, 8, RANK), F32),
            vmem((RANK, RANK), F32),
            vmem((RANK, 2 * RANK), F32),
            vmem((4, RANK, RANK), F32),
            vmem((2, RANK, both), F32),
            vmem((2, RANK, both), F32),
            vmem((2, 6, 32, both), F32),
            vmem((2, 6, 8, both), F32),
            vmem((8, 8, RANK), F32),
            dma((9,)),
            dma((72,)),
            dma((72,)),
            dma((16,)),
            dma((16,)),
            dma((16,)),
            dma((16,)),
            dma((8,)),
            dma((8,)),
        ],
        compiler_params=pltpu.CompilerParams(
            collective_id=0, has_side_effects=True, vmem_limit_bytes=VMEM_LIMIT
        ),
        cost_estimate=pl.CostEstimate(flops=6 * 10**9, bytes_accessed=14 * 2**20, transcendentals=0),
        name="orthonormal",
    )(mom_sq, grad_sq, basis_sq, mom_nw, grad_nw, basis_nw)


def finish_kernel(
    scale_sq, scale_nw,
    mom_sq, grad_sq, mom_nw, grad_nw, left_sq, left_nw, back, squares,
    mom_sq_out, basis_sq_out, upd_sq_out, mom_nw_out, basis_nw_out, upd_nw_out,
    back_hi, back_lo,
):
    k, i = pl.program_id(0), pl.program_id(1)
    wide = mom_sq.shape[2]

    @pl.when(i == 0)
    def _():
        back_hi[...], back_lo[...] = split(back[0])

    def part(which, mom, grad, left, cols, scale, mom_out, upd_out):
        divisor = jnp.sqrt(squares[pl.ds(which, 1), :]) + 1e-06
        pair = (back_hi[:, cols], back_lo[:, cols])
        mom_out[0] = (mom[0] + grad[0].astype(F32)) - (1.0 - MOMENTUM) * dot3(split(left[0]), pair)
        upd_out[0] = (scale * dot3(split(left[0] / divisor), pair)).astype(BF16)
        return divisor

    divisor_sq = part(k, mom_sq, grad_sq, left_sq, slice(0, wide), scale_sq, mom_sq_out, upd_sq_out)
    divisor_nw = part(
        2 + k, mom_nw, grad_nw, left_nw, slice(wide, None), scale_nw, mom_nw_out, upd_nw_out
    )
    n = basis_sq_out.shape[1]
    cols = pl.ds(pl.multiple_of(i * n, n), n)
    basis_sq_out[0] = back[0, :, cols].T / divisor_sq

    @pl.when(i == 0)
    def _():
        basis_nw_out[0] = back[0, :, wide:].T / divisor_nw


def finish(mom_sq, grad_sq, mom_nw, grad_nw, left, back, squares, scale_sq, scale_nw):
    pairs, rows, wide = mom_sq.shape
    thin = mom_nw.shape[2]
    steps = 4
    block = rows // steps

    def by_rows(width, first=0):
        return pl.BlockSpec((1, block, width), lambda k, i: (first + k, i, 0))

    def kernel(*refs):
        finish_kernel(scale_sq, scale_nw, *refs)

    return pl.pallas_call(
        kernel,
        grid=(pairs, steps),
        in_specs=[
            by_rows(wide),
            by_rows(wide),
            by_rows(thin),
            by_rows(thin),
            by_rows(RANK),
            by_rows(RANK, 2),
            pl.BlockSpec((1, RANK, wide + thin), lambda k, i: (k, 0, 0)),
            pl.BlockSpec((8, RANK), lambda k, i: (0, 0)),
        ],
        out_specs=(
            by_rows(wide),
            pl.BlockSpec((1, wide // steps, RANK), lambda k, i: (k, i, 0)),
            by_rows(wide),
            by_rows(thin),
            pl.BlockSpec((1, thin, RANK), lambda k, i: (k, 0, 0)),
            by_rows(thin),
        ),
        out_shape=(
            jax.ShapeDtypeStruct(mom_sq.shape, F32),
            jax.ShapeDtypeStruct((pairs, wide, RANK), F32),
            jax.ShapeDtypeStruct(mom_sq.shape, BF16),
            jax.ShapeDtypeStruct(mom_nw.shape, F32),
            jax.ShapeDtypeStruct((pairs, thin, RANK), F32),
            jax.ShapeDtypeStruct(mom_nw.shape, BF16),
        ),
        scratch_shapes=[
            pltpu.VMEM((RANK, wide + thin), BF16),
            pltpu.VMEM((RANK, wide + thin), BF16),
        ],
        compiler_params=pltpu.CompilerParams(vmem_limit_bytes=VMEM_LIMIT),
        cost_estimate=pl.CostEstimate(flops=4 * 10**9, bytes_accessed=18 * 2**20, transcendentals=0),
        name="finish",
    )(mom_sq, grad_sq, mom_nw, grad_nw, left, left, back, squares)


def local(momentum_square, grad_square, basis_square, momentum_narrow, grad_narrow, basis_narrow):
    left, back, squares = orthonormal(
        momentum_square, grad_square, basis_square, momentum_narrow, grad_narrow, basis_narrow
    )
    total_rows = momentum_square.shape[1] * lax.axis_size("fsdp")
    tp_count = lax.axis_size("tp")
    scale_sq = math.sqrt(total_rows * momentum_square.shape[2] * tp_count / RANK)
    scale_nw = math.sqrt(total_rows * momentum_narrow.shape[2] * tp_count / RANK)
    return finish(
        momentum_square, grad_square, momentum_narrow, grad_narrow, left, back, squares, scale_sq, scale_nw
    )


def solution(mesh):
    by_both = P(None, "fsdp", "tp")
    by_tp = P(None, "tp", None)
    return jax.shard_map(
        local,
        mesh=mesh,
        in_specs=(by_both, by_both, by_tp, by_both, by_both, by_tp),
        out_specs=(by_both, by_tp, by_both, by_both, by_tp, by_both),
        check_vma=False,
    )
```

```python
import math

import jax
import jax.numpy as jnp
from jax import lax
from jax.experimental import pallas as pl
from jax.experimental.pallas import tpu as pltpu
from jax.sharding import PartitionSpec as P

RANK = 256
MOMENTUM = 0.9
MESH = pl.DeviceIdType.MESH
F32 = jnp.float32
BF16 = jnp.bfloat16
PANEL = 32
GROUP = 8
VMEM_LIMIT = 40 * 2**20

RING_X, RING_Y, RING_Z = 4, 4, 4


def split(x):
    hi = x.astype(BF16)
    return hi, (x - hi.astype(F32)).astype(BF16)


def mm(a, b, dims=((1,), (0,))):
    return lax.dot_general(a, b, (dims, ((), ())), preferred_element_type=F32)


def dot3(a, b, dims=((1,), (0,))):
    return mm(a[0], b[0], dims) + (mm(a[0], b[1], dims) + mm(a[1], b[0], dims))


def dot6(a, b, dims=((1,), (0,))):
    return lax.dot_general(
        a, b, (dims, ((), ())), precision=lax.Precision.HIGHEST, preferred_element_type=F32
    )


class Links:
    def __init__(self, send, recv):
        self.send, self.recv, self.sent, self.received = send, recv, 0, 0

    def group(self, ruler):
        return Group(self, ruler)


class Group:
    def __init__(self, links, ruler):
        self.links, self.ruler = links, ruler
        self.sem = links.send.at[links.sent]
        links.sent += 1

    def copy(self, src, dst, device):
        index = self.links.received
        self.links.received += 1
        return pltpu.make_async_remote_copy(
            src_ref=src,
            dst_ref=dst,
            send_sem=self.sem,
            recv_sem=self.links.recv.at[index],
            device_id=device,
            device_id_type=MESH,
        )

    def drain(self):
        pltpu.make_async_copy(self.ruler, self.ruler, self.sem).wait()


class Scatter:
    def __init__(self, links, me, right, left, part, half, inbox):
        self.me, self.part, self.half, self.inbox = me, part, half, inbox
        self.after, self.before = lax.rem(me + 1, 4), lax.rem(me + 3, 4)
        opposite = lax.rem(me + 2, 4)
        self.group = links.group(inbox)

        def outgoing(slot, view, device):
            return self.group.copy(view, inbox.at[slot], device)

        h = half
        self.r1 = outgoing(0, part(opposite, 0, h), right)
        self.r2 = outgoing(1, part(self.after, h, h), right)
        self.r3 = outgoing(2, part(self.after, 0, h), right)
        self.l1 = outgoing(3, part(opposite, h, h), left)
        self.l2 = outgoing(4, part(self.before, 0, h), left)
        self.l3 = outgoing(5, part(self.before, h, h), left)

    def start(self):
        for c in (self.r1, self.l1, self.r2, self.l2):
            c.start()

    def middle(self):
        h = self.half
        self.r1.wait_recv()
        view = self.part(self.after, 0, h)
        view[...] = view[...] + self.inbox[0]
        self.r3.start()
        self.l1.wait_recv()
        view = self.part(self.before, h, h)
        view[...] = view[...] + self.inbox[3]
        self.l3.start()

    def end(self, target):
        h = self.half
        self.r2.wait_recv()
        self.l2.wait_recv()
        self.r3.wait_recv()
        target(0, h)[...] = self.part(self.me, 0, h)[...] + (self.inbox[2] + self.inbox[4])
        self.l3.wait_recv()
        target(h, h)[...] = self.part(self.me, h, h)[...] + (self.inbox[1] + self.inbox[5])


class Gather:
    def __init__(self, links, me, right, left, part, half, ruler):
        after, before = lax.rem(me + 1, 4), lax.rem(me + 3, 4)
        self.group = links.group(ruler)
        h = half

        def outgoing(view, device):
            return self.group.copy(view, view, device)

        self.r1 = outgoing(part(me, 0, 2 * h), right)
        self.l1 = outgoing(part(me, 0, 2 * h), left)
        self.r2 = outgoing(part(before, 0, h), right)
        self.l2 = outgoing(part(after, h, h), left)

    def start(self):
        self.r1.start()
        self.l1.start()

    def middle(self):
        self.r1.wait_recv()
        self.r2.start()
        self.l1.wait_recv()
        self.l2.start()

    def end(self):
        self.r2.wait_recv()
        self.l2.wait_recv()


def factor_block(a):
    rows = lax.broadcasted_iota(jnp.int32, (PANEL, 128), 0)
    done = []
    for s in range(0, PANEL, GROUP):
        n = PANEL - s
        cols = [jnp.broadcast_to(a[s:, s + j : s + j + 1], (n, 128)) for j in range(GROUP)]
        lines = [a[s + j : s + j + 1, :] for j in range(GROUP)]
        rest = a[s + GROUP :]
        for j in range(GROUP):
            pivot = cols[j][j : j + 1, :]
            m = jnp.where(rows[s:] > s + j, cols[j] * (1.0 / pivot), 0.0)
            for q in range(j + 1, GROUP):
                cols[q] = cols[q] - m * cols[q][j : j + 1, :]
            for q in range(j + 1, GROUP):
                lines[q] = lines[q] - m[q : q + 1, :] * lines[j]
            if n > GROUP:
                rest = rest - m[GROUP:] * lines[j]
            done.append(lines[j] * lax.rsqrt(pivot))
        if n > GROUP:
            a = jnp.concatenate([a[: s + GROUP], rest], axis=0)
    return jnp.concatenate(done, axis=0)


def cholesky_start(gram, work):
    n = RANK
    work[:, :n] = gram[...]
    eye = lax.broadcasted_iota(jnp.int32, (n, n), 0) == lax.broadcasted_iota(jnp.int32, (n, n), 1)
    work[:, n:] = eye.astype(F32)


def cholesky_panels(work, inverse, first, last):
    n = RANK
    lane = lax.broadcasted_iota(jnp.int32, (PANEL, 128), 1)
    row = lax.broadcasted_iota(jnp.int32, (PANEL, 128), 0)

    def panel(k, carry):
        off = pl.multiple_of(k * PANEL, PANEL)
        band = work[pl.ds(off, PANEL), :]
        block = pltpu.roll(band[:, :n], lax.rem(n - off, n), axis=1)[:, :128]
        both = jnp.where(lane < PANEL, block, jnp.where(lane == row + PANEL, 1.0, 0.0))
        block_inverse = factor_block(both)[:, PANEL : 2 * PANEL]
        band = dot6(block_inverse, band)
        inverse[pl.ds(off, PANEL), :] = band[:, n:]
        work[...] = work[...] - dot6(band[:, :n], band, ((0,), (0,)))
        return carry

    lax.fori_loop(first, last, panel, 0)


def orthonormal_kernel(
    mom_sq, grad_sq, basis_sq, mom_nw, grad_nw, basis_nw,
    buf_sq, buf_nw, left_out, back_sq, back_nw, squares_out,
    grad_sq_v, basis_sq_v, grad_nw_v, basis_nw_v,
    sq_hi, sq_lo, nw_hi, nw_lo,
    partial, held, projected, scatter_z,
    gram_part, gram_in, gram, chol_work, inverse,
    turned_hi, turned_lo,
    sums_0, sums_1, sums_2, sums_3, wide_0, wide_1, wide_2, wide_3,
    scatter_0, scatter_1, scatter_2, scatter_3, scatter_4, scatter_5, scatter_6, scatter_7,
    norms,
    load_sem, send_sem, recv_sem, gram_sem, norm_sem,
):
    f, t = lax.axis_index("fsdp"), lax.axis_index("tp")
    y, x = f // RING_X, lax.rem(f, RING_X)
    z, core = t // 2, lax.rem(t, 2)
    other = 1 - core
    fsdp_count = RING_X * RING_Y
    tp_count = RING_Z * 2
    links = Links(send_sem, recv_sem)
    gram_ruler = gram_in.at[pl.ds(0, fsdp_count - 1)]

    def at(y=y, x=x, z=z, core=core):
        return (y * RING_X + x, z * 2 + core)

    def step(value, by):
        return lax.rem(value + by, 4)

    sibling = at(core=other)
    x_ring = (x, at(x=step(x, 1)), at(x=step(x, 3)))
    y_ring = (y, at(y=step(y, 1)), at(y=step(y, 3)))
    z_ring = (z, at(z=step(z, 1)), at(z=step(z, 3)))

    barrier = pltpu.get_barrier_semaphore()

    def greet_fsdp(k, carry):
        peer = lax.rem(f + k, fsdp_count)
        pl.semaphore_signal(barrier, inc=1, device_id=(peer, t), device_id_type=MESH)
        return carry

    def greet_tp(k, carry):
        peer = lax.rem(t + k, tp_count)
        pl.semaphore_signal(barrier, inc=1, device_id=(f, peer), device_id_type=MESH)
        return carry

    loads = []

    def load(src, dst):
        c = pltpu.make_async_copy(src, dst, load_sem.at[len(loads)])
        c.start()
        loads.append(c)

    load(basis_nw, basis_nw_v)
    load(mom_nw, buf_nw)
    load(grad_nw, grad_nw_v)
    for k in range(2):
        load(basis_sq.at[k], basis_sq_v.at[k])
        load(mom_sq.at[k], buf_sq.at[k])
        load(grad_sq.at[k], grad_sq_v.at[k])
    lax.fori_loop(1, fsdp_count, greet_fsdp, 0)
    lax.fori_loop(1, tp_count, greet_tp, 0)

    def rows_of(which):
        return pl.ds(pl.multiple_of(which * 256, 256), 256)

    core_group = links.group(held)
    core_copies = [
        core_group.copy(partial.at[i, rows_of(other)], held.at[i], sibling) for i in range(4)
    ]

    def project(i, buf, grad, basis, hi, lo, greeted=True):
        pair = split(basis[...])
        for place, which in enumerate((other, core)):
            rows = rows_of(which)
            b = buf[rows, :] + grad[rows, :].astype(F32)
            buf[rows, :] = b
            b_hi, b_lo = split(b)
            hi[rows, :] = b_hi
            lo[rows, :] = b_lo
            partial[i, rows, :] = dot3((b_hi, b_lo), pair)
            if place == 0:
                if not greeted:
                    pl.semaphore_wait(barrier, fsdp_count + tp_count - 2)
                core_copies[i].start()

    def own_rows(r, i, a, n):
        return projected.at[i, pl.ds(pl.multiple_of(core * 256 + r * 128 + a, 64), n)]

    def held_rows(r):
        return lambda i, a, n: held.at[i, pl.ds(r * 128 + a, n)]

    z_sum = [Scatter(links, *z_ring, held_rows(r), 64, scatter_z.at[r]) for r in range(2)]
    z_all = [
        Gather(links, *z_ring, lambda i, a, n, r=r: own_rows(r, i, a, n), 64, scatter_z.at[r])
        for r in range(2)
    ]
    across_groups = [links.group(partial.at[r]) for r in range(2)]

    def core_send(r, i):
        view = own_rows(r, i, 0, 128)
        return across_groups[r].copy(view, view, sibling)

    across = [[core_send(r, step(z, by)) for by in (0, 3, 1, 2)] for r in range(2)]

    def z_turn(r):
        z_sum[r].end(lambda a, n: own_rows(r, z, a, n))
        z_all[r].start()
        across[r][0].start()

    def z_middle(r):
        z_all[r].middle()
        across[r][1].start()
        across[r][2].start()

    def z_end(r):
        z_all[r].end()
        across[r][3].start()

    for c in loads[:3]:
        c.wait()
    for k in range(2):
        project(
            2 + k, buf_nw.at[k], grad_nw_v.at[k], basis_nw_v.at[k], nw_hi.at[k], nw_lo.at[k], k > 0
        )
    for k in range(2):
        for c in loads[3 + k * 3 : 6 + k * 3]:
            c.wait()
        project(k, buf_sq.at[k], grad_sq_v.at[k], basis_sq_v.at[k], sq_hi.at[k], sq_lo.at[k])
    for i in (2, 3, 0, 1):
        core_copies[i].wait_recv()
        held[i] = held[i] + partial[i, rows_of(core), :]
    for r in range(2):
        z_sum[r].start()
    for r in range(2):
        z_sum[r].middle()
    for r in range(2):
        z_turn(r)

    for r in range(2):
        across[r][0].wait_recv()
    gram_cols = pl.ds(pl.multiple_of(core * 128, 128), 128)
    gram_part[...] = dot6(projected[z, :, gram_cols], projected[z], ((0,), (0,)))

    def gram_rows(i):
        return pl.ds(pl.multiple_of(i * 8, 8), 8)

    def gram_copy(peer, slot):
        return pltpu.make_async_remote_copy(
            src_ref=gram_part.at[gram_rows(peer)],
            dst_ref=gram_in.at[slot],
            send_sem=gram_sem.at[0],
            recv_sem=gram_sem.at[1],
            device_id=(peer, t),
            device_id_type=MESH,
        )

    def full_rows(i):
        return pl.ds(pl.multiple_of(core * 128 + i * 8, 8), 8)

    def gram_copy2(peer):
        view = gram.at[full_rows(f)]
        return pltpu.make_async_remote_copy(
            src_ref=view,
            dst_ref=view,
            send_sem=gram_sem.at[2],
            recv_sem=gram_sem.at[3],
            device_id=(peer, t),
            device_id_type=MESH,
        )

    def gram_wait(which):
        ruler = gram_ruler
        pltpu.make_async_copy(ruler, ruler, gram_sem.at[which]).wait()

    def gram_out(k, carry):
        gram_copy(lax.rem(f + k, fsdp_count), f).start()
        return carry

    def gram_out2(k, carry):
        gram_copy2(lax.rem(f + k, fsdp_count)).start()
        return carry

    lax.fori_loop(1, fsdp_count, gram_out, 0)
    z_middle(0)
    z_middle(1)
    gram_wait(1)
    gram_in[f] = gram_part[gram_rows(f), :]
    gram[full_rows(f), :] = jnp.sum(gram_in[...], axis=0)
    lax.fori_loop(1, fsdp_count, gram_out2, 0)
    z_end(0)
    z_end(1)
    gram_wait(3)
    half_rows = gram.at[pl.ds(pl.multiple_of(core * 128, 128), 128)]
    gram_across_group = links.group(half_rows)
    gram_across = gram_across_group.copy(half_rows, half_rows, sibling)
    gram_across.start()

    sums = (sums_0, sums_1, sums_2, sums_3)
    wides = (wide_0, wide_1, wide_2, wide_3)
    inboxes = (scatter_0, scatter_1, scatter_2, scatter_3)
    inboxes_2 = (scatter_4, scatter_5, scatter_6, scatter_7)
    outer = (x_ring, y_ring, x_ring, y_ring)
    inner = (y_ring, x_ring, y_ring, x_ring)

    def thick(ref):
        return lambda i, a, n: ref.at[pl.ds(pl.multiple_of(i * 64 + a, 32), n)]

    def thin(ref, p):
        place = outer[p][0] * 64
        return lambda i, a, n: ref.at[pl.ds(pl.multiple_of(place + i * 16 + a, 8), n)]

    sum_1 = [Scatter(links, *outer[p], thick(sums[p]), 32, inboxes[p]) for p in range(4)]
    sum_2 = [Scatter(links, *inner[p], thin(sums[p], p), 8, inboxes_2[p]) for p in range(4)]
    all_1 = [Gather(links, *inner[p], thin(wides[p], p), 8, inboxes_2[p]) for p in range(4)]
    all_2 = [Gather(links, *outer[p], thick(wides[p]), 32, inboxes[p]) for p in range(4)]

    def sum_1_end(p):
        sum_1[p].end(lambda a, n: thick(sums[p])(outer[p][0], a, n))
        sum_2[p].start()

    def sum_2_end(p):
        sum_2[p].end(lambda a, n: thin(wides[p], p)(inner[p][0], a, n))
        all_1[p].start()

    def all_1_end(p):
        all_1[p].end()
        all_2[p].start()

    half_cols = sq_hi.shape[2] // 2

    def narrow_back(k):
        sums[k][:, half_cols:] = dot3(split(projected[2 + k].T), (nw_hi[k], nw_lo[k]))

    def square_back(k):
        turned_hi[...], turned_lo[...] = split(projected[k].T)
        for h in range(2):
            cols = slice(h * half_cols, (h + 1) * half_cols)
            part = dot3((turned_hi[...], turned_lo[...]), (sq_hi[k, :, cols], sq_lo[k, :, cols]))
            sums[2 * k + h][:, :half_cols] = part
            sum_1[2 * k + h].start()

    for r in range(2):
        for c in across[r][1:]:
            c.wait_recv()
    narrow_back(0)
    narrow_back(1)
    square_back(0)
    square_back(1)

    gram_across.wait_recv()
    own_inverse = inverse.at[z]
    cholesky_start(gram, chol_work)

    class Band:
        def __init__(self, first, rows):
            share = rows // 2

            def part(i, a, n):
                row = pl.multiple_of(first + core * share + a, 16)
                return inverse.at[i, pl.ds(row, n)]

            ruler = partial.at[0, pl.ds(0, 3 * share)]
            self.ring = Gather(links, *z_ring, part, share // 2, ruler)
            self.group = links.group(ruler)
            views = [part(step(z, by), 0, share) for by in (3, 1, 2)]
            self.across = [self.group.copy(v, v, sibling) for v in views]

        def start(self):
            self.ring.start()

        def middle(self):
            self.ring.middle()
            self.across[0].start()
            self.across[1].start()

        def end(self):
            self.ring.end()
            self.across[2].start()

        def wait(self):
            for c in self.across:
                c.wait_recv()

    bands = [Band(0, 192), Band(192, 64)]

    def panels(first, last):
        cholesky_panels(chol_work, own_inverse, first, last)

    panels(0, 2)
    for p in (0, 1, 2, 3):
        sum_1[p].middle()
    panels(2, 4)
    for p in (0, 1):
        sum_1_end(p)
    panels(4, 5)
    for p in (2, 3):
        sum_1_end(p)
    for p in (0, 1):
        sum_2[p].middle()
    panels(5, 6)
    for p in (0, 1):
        sum_2_end(p)
    for p in (2, 3):
        sum_2[p].middle()
    panels(6, 7)
    for p in (0, 1):
        all_1[p].middle()
    for p in (2, 3):
        sum_2_end(p)
    for p in (0, 1):
        all_1_end(p)
    panels(7, 8)
    bands[0].start()
    bands[1].start()
    for p in (2, 3):
        all_1[p].middle()
    for p in (2, 3):
        all_1_end(p)
    bands[0].middle()
    bands[1].middle()
    for p in (0, 1):
        all_2[p].middle()
    bands[0].end()
    bands[1].end()
    for p in (2, 3):
        all_2[p].middle()
    bands[0].wait()
    bands[1].wait()

    for i in range(4):
        left_out[i] = dot3(split(projected[i]), split(inverse[i]), ((1,), (1,)))

    norms[t] = jnp.zeros((8, RANK), F32)

    def back_factor(i, source, target):
        back = dot3(split(inverse[i]), split(source))
        target[...] = back
        square = jnp.sum(back * back, axis=1, keepdims=True)
        square = jnp.broadcast_to(square, (RANK, 128)).T
        norms[t, pl.ds(i, 1), :] = norms[t, pl.ds(i, 1), :] + square[:1]

    for p in range(4):
        all_2[p].end()
        k, h = p // 2, p % 2
        cols = slice(h * half_cols, (h + 1) * half_cols)
        back_factor(k, wides[p][:, :half_cols], back_sq.at[k, :, cols])
        if k == 0:
            back_factor(2 + h, wides[p][:, half_cols:], back_nw.at[h])

    def norm_copy(peer):
        return pltpu.make_async_remote_copy(
            src_ref=norms.at[t],
            dst_ref=norms.at[t],
            send_sem=norm_sem.at[0],
            recv_sem=norm_sem.at[1],
            device_id=(f, peer),
            device_id_type=MESH,
        )

    def norm_wait(which):
        ruler = norms.at[pl.ds(0, tp_count - 1)]
        pltpu.make_async_copy(ruler, ruler, norm_sem.at[which]).wait()

    def norm_out(k, carry):
        norm_copy(lax.rem(t + k, tp_count)).start()
        return carry

    lax.fori_loop(1, tp_count, norm_out, 0)

    for group in [core_group, gram_across_group] + across_groups:
        group.drain()
    for band in bands:
        band.ring.group.drain()
        band.group.drain()
    for ring in z_sum + z_all + sum_1 + sum_2 + all_1 + all_2:
        ring.group.drain()
    gram_wait(0)
    gram_wait(2)
    norm_wait(1)
    squares_out[...] = jnp.sum(norms[...], axis=0)
    norm_wait(0)


def orthonormal(*args):
    mom_sq, grad_sq, basis_sq, mom_nw, grad_nw, basis_nw = args
    rows = mom_sq.shape[1]
    wide, thin = mom_sq.shape[2], mom_nw.shape[2]
    widths = (wide // 2 + thin, wide // 2 + thin, wide // 2, wide // 2)
    vmem = pltpu.VMEM
    dma = pltpu.SemaphoreType.DMA
    whole = pl.BlockSpec(memory_space=pltpu.VMEM)
    return pl.pallas_call(
        orthonormal_kernel,
        out_shape=(
            pltpu.VMEM(mom_sq.shape, F32),
            pltpu.VMEM(mom_nw.shape, F32),
            pltpu.VMEM((4, rows, RANK), F32),
            pltpu.VMEM((2, RANK, wide), F32),
            pltpu.VMEM((2, RANK, thin), F32),
            pltpu.VMEM((8, RANK), F32),
        ),
        in_specs=[pl.BlockSpec(memory_space=pltpu.HBM)] * 6,
        out_specs=(whole,) * 6,
        scratch_shapes=[
            vmem(grad_sq.shape, BF16),
            vmem(basis_sq.shape, F32),
            vmem(grad_nw.shape, BF16),
            vmem(basis_nw.shape, F32),
            vmem(mom_sq.shape, BF16),
            vmem(mom_sq.shape, BF16),
            vmem(mom_nw.shape, BF16),
            vmem(mom_nw.shape, BF16),
            vmem((4, rows, RANK), F32),
            vmem((4, rows // 2, RANK), F32),
            vmem((4, rows, RANK), F32),
            vmem((2, 6, rows // 8, RANK), F32),
            vmem((128, RANK), F32),
            vmem((16, 8, RANK), F32),
            vmem((RANK, RANK), F32),
            vmem((RANK, 2 * RANK), F32),
            vmem((4, RANK, RANK), F32),
            vmem((RANK, rows), BF16),
            vmem((RANK, rows), BF16),
            *[vmem((RANK, w), F32) for w in widths],
            *[vmem((RANK, w), F32) for w in widths],
            *[vmem((6, 32, w), F32) for w in widths],
            *[vmem((6, 8, w), F32) for w in widths],
            vmem((8, 8, RANK), F32),
            dma((9,)),
            dma((28,)),
            dma((127,)),
            dma((4,)),
            dma((2,)),
        ],
        compiler_params=pltpu.CompilerParams(
            collective_id=0, has_side_effects=True, vmem_limit_bytes=VMEM_LIMIT
        ),
        cost_estimate=pl.CostEstimate(flops=6 * 10**9, bytes_accessed=9 * 2**20, transcendentals=0),
        name="orthonormal",
    )(*(pltpu.with_memory_space_constraint(a, pltpu.HBM) for a in args))


def finish_kernel(
    scale_sq, scale_nw,
    buf_sq, buf_nw, left, back_sq, back_nw, squares,
    mom_sq_out, basis_sq_out, upd_sq_out, mom_nw_out, basis_nw_out, upd_nw_out,
    mom_sq, basis_sq, upd_sq, mom_nw, basis_nw, upd_nw, store_sem,
):
    rows = buf_sq.shape[1]
    pieces = 2
    piece = rows // pieces
    stores = []

    def store(src, dst):
        c = pltpu.make_async_copy(src, dst, store_sem.at[len(stores)])
        c.start()
        stores.append(c)

    def part(mom, upd, buf, factor, pair, divisor, scale):
        mom[...] = buf - mm((factor * (1.0 - MOMENTUM)).astype(BF16), pair[0])
        upd[...] = (scale * dot3(split(factor / divisor), pair)).astype(BF16)

    for k in range(2):
        divisor_sq, divisor_nw = (
            jnp.sqrt(squares[i : i + 1, :]) + 1e-06 for i in (k, 2 + k)
        )
        basis_sq[k] = back_sq[k].T / divisor_sq
        store(basis_sq.at[k], basis_sq_out.at[k])
        pair = split(back_sq[k])
        for p in range(pieces):
            r = pl.ds(p * piece, piece)
            part(mom_sq.at[k, r], upd_sq.at[k, r], buf_sq[k, r, :], left[k, r, :], pair, divisor_sq, scale_sq)
            store(mom_sq.at[k, r], mom_sq_out.at[k, r])
            store(upd_sq.at[k, r], upd_sq_out.at[k, r])
        basis_nw[k] = back_nw[k].T / divisor_nw
        part(mom_nw.at[k], upd_nw.at[k], buf_nw[k], left[2 + k], split(back_nw[k]), divisor_nw, scale_nw)
        store(mom_nw.at[k], mom_nw_out.at[k])
        store(basis_nw.at[k], basis_nw_out.at[k])
        store(upd_nw.at[k], upd_nw_out.at[k])
    for c in stores:
        c.wait()


def finish(buf_sq, buf_nw, left, back_sq, back_nw, squares, scale_sq, scale_nw):
    pairs, rows, wide = buf_sq.shape
    thin = buf_nw.shape[2]
    outs = (
        jax.ShapeDtypeStruct(buf_sq.shape, F32),
        jax.ShapeDtypeStruct((pairs, wide, RANK), F32),
        jax.ShapeDtypeStruct(buf_sq.shape, BF16),
        jax.ShapeDtypeStruct(buf_nw.shape, F32),
        jax.ShapeDtypeStruct((pairs, thin, RANK), F32),
        jax.ShapeDtypeStruct(buf_nw.shape, BF16),
    )

    def kernel(*refs):
        finish_kernel(scale_sq, scale_nw, *refs)

    return pl.pallas_call(
        kernel,
        out_shape=outs,
        in_specs=[pl.BlockSpec(memory_space=pltpu.VMEM)] * 6,
        out_specs=(pl.BlockSpec(memory_space=pltpu.HBM),) * 6,
        scratch_shapes=[pltpu.VMEM(o.shape, o.dtype) for o in outs]
        + [pltpu.SemaphoreType.DMA((16,))],
        compiler_params=pltpu.CompilerParams(vmem_limit_bytes=VMEM_LIMIT),
        cost_estimate=pl.CostEstimate(flops=3 * 10**9, bytes_accessed=9 * 2**20, transcendentals=0),
        name="finish",
    )(buf_sq, buf_nw, left, back_sq, back_nw, squares)


def local(momentum_square, grad_square, basis_square, momentum_narrow, grad_narrow, basis_narrow):
    parts = orthonormal(
        momentum_square, grad_square, basis_square, momentum_narrow, grad_narrow, basis_narrow
    )
    total_rows = momentum_square.shape[1] * lax.axis_size("fsdp")
    tp_count = lax.axis_size("tp")
    scale_sq = math.sqrt(total_rows * momentum_square.shape[2] * tp_count / RANK)
    scale_nw = math.sqrt(total_rows * momentum_narrow.shape[2] * tp_count / RANK)
    return finish(*parts, scale_sq, scale_nw)


def solution(mesh):
    by_both = P(None, "fsdp", "tp")
    by_tp = P(None, "tp", None)
    return jax.shard_map(
        local,
        mesh=mesh,
        in_specs=(by_both, by_both, by_tp, by_both, by_both, by_tp),
        out_specs=(by_both, by_tp, by_both, by_both, by_tp, by_both),
        check_vma=False,
    )
```

```python
import math

import jax
import jax.numpy as jnp
from jax import lax
from jax.experimental import pallas as pl
from jax.experimental.pallas import tpu as pltpu
from jax.sharding import PartitionSpec as P

RANK = 256
MOMENTUM = 0.9
MESH = pl.DeviceIdType.MESH
F32 = jnp.float32
BF16 = jnp.bfloat16
PANEL = 32
GROUP = 8
VMEM_LIMIT = 40 * 2**20

RING_X, RING_Y, RING_Z = 4, 4, 4


def split(x):
    hi = x.astype(BF16)
    return hi, (x - hi.astype(F32)).astype(BF16)


def mm(a, b, dims=((1,), (0,))):
    return lax.dot_general(a, b, (dims, ((), ())), preferred_element_type=F32)


def dot3(a, b, dims=((1,), (0,))):
    return mm(a[0], b[0], dims) + (mm(a[0], b[1], dims) + mm(a[1], b[0], dims))


def dot6(a, b, dims=((1,), (0,))):
    return lax.dot_general(
        a, b, (dims, ((), ())), precision=lax.Precision.HIGHEST, preferred_element_type=F32
    )


class Links:
    def __init__(self, send, recv):
        self.send, self.recv, self.sent, self.received = send, recv, 0, 0

    def group(self, ruler):
        return Group(self, ruler)


class Group:
    def __init__(self, links, ruler):
        self.links, self.ruler = links, ruler
        self.sem = links.send.at[links.sent]
        links.sent += 1

    def copy(self, src, dst, device):
        index = self.links.received
        self.links.received += 1
        return pltpu.make_async_remote_copy(
            src_ref=src,
            dst_ref=dst,
            send_sem=self.sem,
            recv_sem=self.links.recv.at[index],
            device_id=device,
            device_id_type=MESH,
        )

    def drain(self):
        pltpu.make_async_copy(self.ruler, self.ruler, self.sem).wait()


class Scatter:
    def __init__(self, links, me, right, left, part, half, inbox):
        self.me, self.part, self.half, self.inbox = me, part, half, inbox
        self.after, self.before = lax.rem(me + 1, 4), lax.rem(me + 3, 4)
        opposite = lax.rem(me + 2, 4)
        self.group = links.group(inbox)

        def outgoing(slot, view, device):
            return self.group.copy(view, inbox.at[slot], device)

        h = half
        self.r1 = outgoing(0, part(opposite, 0, h), right)
        self.r2 = outgoing(1, part(self.after, h, h), right)
        self.r3 = outgoing(2, part(self.after, 0, h), right)
        self.l1 = outgoing(3, part(opposite, h, h), left)
        self.l2 = outgoing(4, part(self.before, 0, h), left)
        self.l3 = outgoing(5, part(self.before, h, h), left)

    def start(self):
        self.r1.start()
        self.l1.start()

    def start_rest(self):
        self.r2.start()
        self.l2.start()

    def middle(self):
        h = self.half
        self.r1.wait_recv()
        view = self.part(self.after, 0, h)
        view[...] = view[...] + self.inbox[0]
        self.r3.start()
        self.l1.wait_recv()
        view = self.part(self.before, h, h)
        view[...] = view[...] + self.inbox[3]
        self.l3.start()

    def end(self, target):
        h = self.half
        self.r2.wait_recv()
        self.l2.wait_recv()
        self.r3.wait_recv()
        target(0, h)[...] = self.part(self.me, 0, h)[...] + (self.inbox[2] + self.inbox[4])
        self.l3.wait_recv()
        target(h, h)[...] = self.part(self.me, h, h)[...] + (self.inbox[1] + self.inbox[5])


class Gather:
    def __init__(self, links, me, right, left, part, half, ruler):
        after, before = lax.rem(me + 1, 4), lax.rem(me + 3, 4)
        self.group = links.group(ruler)
        h = half

        def outgoing(view, device):
            return self.group.copy(view, view, device)

        self.r1 = outgoing(part(me, 0, 2 * h), right)
        self.l1 = outgoing(part(me, 0, 2 * h), left)
        self.r2 = outgoing(part(before, 0, h), right)
        self.l2 = outgoing(part(after, h, h), left)

    def start(self):
        self.r1.start()
        self.l1.start()

    def middle(self):
        self.r1.wait_recv()
        self.r2.start()
        self.l1.wait_recv()
        self.l2.start()

    def end(self):
        self.r2.wait_recv()
        self.l2.wait_recv()


class DirectScatter:
    def __init__(self, links, me, device_of, part, rows, inbox):
        self.me, self.part, self.rows, self.inbox = me, part, rows, inbox
        self.group = links.group(inbox)
        self.copies = []
        for by in (2, 1, 3):
            peer = lax.rem(me + by, 4)
            view = part(peer, 0, rows)
            self.copies.append(self.group.copy(view, inbox.at[by - 1], device_of(peer)))

    def start(self):
        for c in self.copies:
            c.start()

    def end(self, target):
        for c in self.copies:
            c.wait_recv()
        own = self.part(self.me, 0, self.rows)[...]
        target(0, self.rows)[...] = (own + self.inbox[0]) + (self.inbox[1] + self.inbox[2])


class DirectGather:
    def __init__(self, links, me, device_of, part, rows, ruler):
        self.group = links.group(ruler)
        view = part(me, 0, rows)
        self.copies = [
            self.group.copy(view, view, device_of(lax.rem(me + by, 4))) for by in (2, 1, 3)
        ]

    def start(self):
        for c in self.copies:
            c.start()

    def end(self):
        for c in self.copies:
            c.wait_recv()


def factor_block(a):
    rows = lax.broadcasted_iota(jnp.int32, (PANEL, 128), 0)
    done = []
    for s in range(0, PANEL, GROUP):
        n = PANEL - s
        cols = [jnp.broadcast_to(a[s:, s + j : s + j + 1], (n, 128)) for j in range(GROUP)]
        lines = [a[s + j : s + j + 1, :] for j in range(GROUP)]
        rest = a[s + GROUP :]
        for j in range(GROUP):
            pivot = cols[j][j : j + 1, :]
            m = jnp.where(rows[s:] > s + j, cols[j] * (1.0 / pivot), 0.0)
            for q in range(j + 1, GROUP):
                cols[q] = cols[q] - m * cols[q][j : j + 1, :]
            for q in range(j + 1, GROUP):
                lines[q] = lines[q] - m[q : q + 1, :] * lines[j]
            if n > GROUP:
                rest = rest - m[GROUP:] * lines[j]
            done.append(lines[j] * lax.rsqrt(pivot))
        if n > GROUP:
            a = jnp.concatenate([a[: s + GROUP], rest], axis=0)
    return jnp.concatenate(done, axis=0)


def cholesky_start(gram, work):
    n = RANK
    work[:, :n] = gram[...]
    eye = lax.broadcasted_iota(jnp.int32, (n, n), 0) == lax.broadcasted_iota(jnp.int32, (n, n), 1)
    work[:, n:] = eye.astype(F32)


def cholesky_panels(work, inverse, first, last):
    n = RANK
    lane = lax.broadcasted_iota(jnp.int32, (PANEL, 128), 1)
    row = lax.broadcasted_iota(jnp.int32, (PANEL, 128), 0)

    def panel(k, carry):
        off = pl.multiple_of(k * PANEL, PANEL)
        band = work[pl.ds(off, PANEL), :]
        block = pltpu.roll(band[:, :n], lax.rem(n - off, n), axis=1)[:, :128]
        both = jnp.where(lane < PANEL, block, jnp.where(lane == row + PANEL, 1.0, 0.0))
        block_inverse = factor_block(both)[:, PANEL : 2 * PANEL]
        band = dot6(block_inverse, band)
        inverse[pl.ds(off, PANEL), :] = band[:, n:]
        work[...] = work[...] - dot6(band[:, :n], band, ((0,), (0,)))
        return carry

    lax.fori_loop(first, last, panel, 0)


def orthonormal_kernel(
    mom_sq, grad_sq, basis_sq, mom_nw, grad_nw, basis_nw,
    buf_sq, buf_nw, left_out, back_sq, back_nw, squares_out,
    grad_sq_v, basis_sq_v, grad_nw_v, basis_nw_v,
    sq_hi, sq_lo, nw_hi, nw_lo,
    partial, held, projected, scatter_z,
    gram_part, gram_in, gram, chol_work, inverse,
    turned_hi, turned_lo,
    sums_0, sums_1, sums_2, sums_3, wide_0, wide_1, wide_2, wide_3,
    scatter_0, scatter_1, scatter_2, scatter_3, scatter_4, scatter_5, scatter_6, scatter_7,
    norms, rulers,
    load_sem, send_sem, recv_sem, gram_sem, norm_sem,
):
    f, t = lax.axis_index("fsdp"), lax.axis_index("tp")
    y, x = f // RING_X, lax.rem(f, RING_X)
    z, core = t // 2, lax.rem(t, 2)
    other = 1 - core
    fsdp_count = RING_X * RING_Y
    tp_count = RING_Z * 2
    links = Links(send_sem, recv_sem)
    gram_ruler = gram_in.at[pl.ds(0, fsdp_count - 1)]

    def at(y=y, x=x, z=z, core=core):
        return (y * RING_X + x, z * 2 + core)

    def step(value, by):
        return lax.rem(value + by, 4)

    sibling = at(core=other)
    x_ring = (x, at(x=step(x, 1)), at(x=step(x, 3)))
    y_ring = (y, at(y=step(y, 1)), at(y=step(y, 3)))
    z_ring = (z, at(z=step(z, 1)), at(z=step(z, 3)))

    barrier = pltpu.get_barrier_semaphore()

    def greet_fsdp(k, carry):
        peer = lax.rem(f + k, fsdp_count)
        pl.semaphore_signal(barrier, inc=1, device_id=(peer, t), device_id_type=MESH)
        return carry

    def greet_tp(k, carry):
        peer = lax.rem(t + k, tp_count)
        pl.semaphore_signal(barrier, inc=1, device_id=(f, peer), device_id_type=MESH)
        return carry

    loads = []

    def load(src, dst):
        c = pltpu.make_async_copy(src, dst, load_sem.at[len(loads)])
        c.start()
        loads.append(c)

    load(basis_nw, basis_nw_v)
    load(mom_nw, buf_nw)
    load(grad_nw, grad_nw_v)
    for k in range(2):
        load(basis_sq.at[k], basis_sq_v.at[k])
        load(mom_sq.at[k], buf_sq.at[k])
        load(grad_sq.at[k], grad_sq_v.at[k])
    lax.fori_loop(1, fsdp_count, greet_fsdp, 0)
    lax.fori_loop(1, tp_count, greet_tp, 0)

    def rows_of(which):
        return pl.ds(pl.multiple_of(which * 256, 256), 256)

    core_group = links.group(held)
    core_copies = [
        core_group.copy(partial.at[i, rows_of(other)], held.at[i], sibling) for i in range(4)
    ]

    def project(i, buf, grad, basis, hi, lo, greeted=True):
        pair = split(basis[...])
        for place, which in enumerate((other, core)):
            rows = rows_of(which)
            b = buf[rows, :] + grad[rows, :].astype(F32)
            buf[rows, :] = b
            b_hi, b_lo = split(b)
            hi[rows, :] = b_hi
            lo[rows, :] = b_lo
            partial[i, rows, :] = dot3((b_hi, b_lo), pair)
            if place == 0:
                if not greeted:
                    pl.semaphore_wait(barrier, fsdp_count + tp_count - 2)
                core_copies[i].start()

    def own_rows(r, i, a, n):
        return projected.at[i, pl.ds(pl.multiple_of(core * 256 + r * 128 + a, 64), n)]

    def held_rows(r):
        return lambda i, a, n: held.at[i, pl.ds(r * 128 + a, n)]

    z_sum = [Scatter(links, *z_ring, held_rows(r), 64, scatter_z.at[r]) for r in range(2)]
    z_all = [
        Gather(links, *z_ring, lambda i, a, n, r=r: own_rows(r, i, a, n), 64, scatter_z.at[r])
        for r in range(2)
    ]
    across_groups = [links.group(partial.at[r]) for r in range(2)]

    def core_send(r, i):
        view = own_rows(r, i, 0, 128)
        return across_groups[r].copy(view, view, sibling)

    across = [[core_send(r, step(z, by)) for by in (0, 3, 1, 2)] for r in range(2)]

    def z_wait(r):
        for c in across[r][1:]:
            c.wait_recv()

    def z_turn(r):
        z_sum[r].end(lambda a, n: own_rows(r, z, a, n))
        z_all[r].start()
        across[r][0].start()

    def z_middle(r):
        z_all[r].middle()
        across[r][1].start()
        across[r][2].start()

    def z_end(r):
        z_all[r].end()
        across[r][3].start()

    for c in loads[:3]:
        c.wait()
    for k in range(2):
        project(
            2 + k, buf_nw.at[k], grad_nw_v.at[k], basis_nw_v.at[k], nw_hi.at[k], nw_lo.at[k], k > 0
        )
    for k in range(2):
        for c in loads[3 + k * 3 : 6 + k * 3]:
            c.wait()
        project(k, buf_sq.at[k], grad_sq_v.at[k], basis_sq_v.at[k], sq_hi.at[k], sq_lo.at[k])
    for i in (2, 3, 0, 1):
        core_copies[i].wait_recv()
        held[i] = held[i] + partial[i, rows_of(core), :]
    z_sum[0].start()
    z_sum[0].start_rest()
    z_sum[1].start()
    z_sum[0].middle()
    z_sum[1].start_rest()
    z_sum[1].middle()
    z_turn(0)
    z_turn(1)

    def gram_rows(i):
        return pl.ds(pl.multiple_of(i * 8, 8), 8)

    def gram_copy(peer, slot):
        return pltpu.make_async_remote_copy(
            src_ref=gram_part.at[gram_rows(peer)],
            dst_ref=gram_in.at[slot],
            send_sem=gram_sem.at[0],
            recv_sem=gram_sem.at[1],
            device_id=(peer, t),
            device_id_type=MESH,
        )

    def full_rows(i):
        return pl.ds(pl.multiple_of(core * 128 + i * 8, 8), 8)

    def gram_copy2(peer):
        view = gram.at[full_rows(f)]
        return pltpu.make_async_remote_copy(
            src_ref=view,
            dst_ref=view,
            send_sem=gram_sem.at[2],
            recv_sem=gram_sem.at[3],
            device_id=(peer, t),
            device_id_type=MESH,
        )

    def gram_wait(which):
        ruler = gram_ruler
        pltpu.make_async_copy(ruler, ruler, gram_sem.at[which]).wait()

    def gram_out(k, carry):
        gram_copy(lax.rem(f + k, fsdp_count), f).start()
        return carry

    def gram_out2(k, carry):
        gram_copy2(lax.rem(f + k, fsdp_count)).start()
        return carry

    sums = (sums_0, sums_1, sums_2, sums_3)
    wides = (wide_0, wide_1, wide_2, wide_3)
    inboxes = (scatter_0, scatter_1, scatter_2, scatter_3)
    inboxes_2 = (scatter_4, scatter_5, scatter_6, scatter_7)
    outer = (x_ring, y_ring, x_ring, y_ring)
    inner = (y_ring, x_ring, y_ring, x_ring)

    def thick(ref):
        return lambda i, a, n: ref.at[pl.ds(pl.multiple_of(i * 64 + a, 32), n)]

    def thin(ref, p):
        place = outer[p][0] * 64
        return lambda i, a, n: ref.at[pl.ds(pl.multiple_of(place + i * 16 + a, 16), n)]

    sum_1 = [Scatter(links, *outer[p], thick(sums[p]), 32, inboxes[p]) for p in range(4)]
    def on_x(i):
        return at(x=i)

    def on_y(i):
        return at(y=i)

    across_of = (on_y, on_x, on_y, on_x)
    sum_2 = [
        DirectScatter(links, inner[p][0], across_of[p], thin(sums[p], p), 16, inboxes_2[p])
        for p in range(4)
    ]
    all_1 = [
        DirectGather(links, inner[p][0], across_of[p], thin(wides[p], p), 16, inboxes_2[p])
        for p in range(4)
    ]
    all_2 = [Gather(links, *outer[p], thick(wides[p]), 32, inboxes[p]) for p in range(4)]

    def sum_1_end(p):
        sum_1[p].end(lambda a, n: thick(sums[p])(outer[p][0], a, n))
        sum_2[p].start()

    def sum_2_end(p):
        sum_2[p].end(lambda a, n: thin(wides[p], p)(inner[p][0], a, n))
        all_1[p].start()

    def all_1_end(p):
        all_1[p].end()
        all_2[p].start()

    half_cols = sq_hi.shape[2] // 2

    def narrow_back(k):
        factor = split(projected[2 + k].T)
        sums[3 * k][:, half_cols:] = dot3(factor, (nw_hi[k], nw_lo[k]))

    def square_back(k):
        turned_hi[...], turned_lo[...] = split(projected[k].T)
        for h in range(2):
            cols = slice(h * half_cols, (h + 1) * half_cols)
            part = dot3((turned_hi[...], turned_lo[...]), (sq_hi[k, :, cols], sq_lo[k, :, cols]))
            sums[2 * k + h][:, :half_cols] = part
            sum_1[2 * k + h].start()
            if k == 0:
                sum_1[h].start_rest()

    for r in range(2):
        across[r][0].wait_recv()
    gram_cols = pl.ds(pl.multiple_of(core * 128, 128), 128)
    gram_part[...] = dot6(projected[z, :, gram_cols], projected[z], ((0,), (0,)))
    lax.fori_loop(1, fsdp_count, gram_out, 0)
    z_middle(0)
    gram_wait(1)
    gram_in[f] = gram_part[gram_rows(f), :]
    gram[full_rows(f), :] = jnp.sum(gram_in[...], axis=0)
    lax.fori_loop(1, fsdp_count, gram_out2, 0)
    z_middle(1)
    gram_wait(3)
    half_rows = gram.at[pl.ds(pl.multiple_of(core * 128, 128), 128)]
    gram_across_group = links.group(half_rows)
    gram_across = gram_across_group.copy(half_rows, half_rows, sibling)
    gram_across.start()
    z_end(0)
    gram_across.wait_recv()

    own_inverse = inverse.at[z]
    cholesky_start(gram, chol_work)

    class Band:
        def __init__(self, first, rows):
            share = rows // 2

            def part(i, a, n):
                row = pl.multiple_of(first + core * share + a, 16)
                return inverse.at[i, pl.ds(row, n)]

            ruler = rulers.at[pl.ds(0, 3 * share)]
            self.ring = Gather(links, *z_ring, part, share // 2, ruler)
            self.group = links.group(ruler)
            views = [part(step(z, by), 0, share) for by in (3, 1, 2)]
            self.across = [self.group.copy(v, v, sibling) for v in views]

        def start(self):
            self.ring.start()

        def middle(self):
            self.ring.middle()
            self.across[0].start()
            self.across[1].start()

        def end(self):
            self.ring.end()
            self.across[2].start()

        def wait(self):
            for c in self.across:
                c.wait_recv()

    bands = [Band(0, 192), Band(192, 64)]

    def panels(first, last):
        cholesky_panels(chol_work, own_inverse, first, last)

    panels(0, 1)
    z_end(1)
    z_wait(0)
    z_wait(1)
    narrow_back(0)
    square_back(0)
    narrow_back(1)
    square_back(1)
    panels(1, 3)
    for p in (0, 1):
        sum_1[p].middle()
    for p in (2, 3):
        sum_1[p].start_rest()
    panels(3, 4)
    for p in (2, 3):
        sum_1[p].middle()
    panels(4, 6)
    for p in (0, 1):
        sum_1_end(p)
    panels(6, 7)
    for p in (2, 3):
        sum_1_end(p)
    for p in (0, 1):
        sum_2_end(p)
    panels(7, 8)
    bands[0].start()
    bands[1].start()
    for p in (2, 3):
        sum_2_end(p)
    for p in (0, 1):
        all_1_end(p)
    bands[0].middle()
    bands[1].middle()
    for p in (2, 3):
        all_1_end(p)
    for p in (0, 1):
        all_2[p].middle()
    bands[0].end()
    bands[1].end()
    for p in (2, 3):
        all_2[p].middle()
    bands[0].wait()
    bands[1].wait()

    norms[t] = jnp.zeros((8, RANK), F32)

    def back_factor(i, source, target):
        back = dot3(split(inverse[i]), split(source))
        target[...] = back
        square = jnp.sum(back * back, axis=1, keepdims=True)
        square = jnp.broadcast_to(square, (RANK, 128)).T
        norms[t, pl.ds(i, 1), :] = norms[t, pl.ds(i, 1), :] + square[:1]

    def back_factors(p):
        all_2[p].end()
        k, h = p // 2, p % 2
        cols = slice(h * half_cols, (h + 1) * half_cols)
        back_factor(k, wides[p][:, :half_cols], back_sq.at[k, :, cols])
        if k == h:
            back_factor(2 + k, wides[p][:, half_cols:], back_nw.at[k])

    def left_factor(i):
        left_out[i] = dot3(split(projected[i]), split(inverse[i]), ((1,), (1,)))

    for i in range(4):
        left_factor(i)
    back_factors(0)
    back_factors(1)
    back_factors(2)
    back_factors(3)

    def norm_copy(peer):
        return pltpu.make_async_remote_copy(
            src_ref=norms.at[t],
            dst_ref=norms.at[t],
            send_sem=norm_sem.at[0],
            recv_sem=norm_sem.at[1],
            device_id=(f, peer),
            device_id_type=MESH,
        )

    def norm_wait(which):
        ruler = norms.at[pl.ds(0, tp_count - 1)]
        pltpu.make_async_copy(ruler, ruler, norm_sem.at[which]).wait()

    def norm_out(k, carry):
        norm_copy(lax.rem(t + k, tp_count)).start()
        return carry

    lax.fori_loop(1, tp_count, norm_out, 0)

    for group in [core_group, gram_across_group] + across_groups:
        group.drain()
    for band in bands:
        band.ring.group.drain()
        band.group.drain()
    for ring in z_sum + z_all + sum_1 + sum_2 + all_1 + all_2:
        ring.group.drain()
    gram_wait(0)
    gram_wait(2)
    norm_wait(1)
    squares_out[...] = jnp.sum(norms[...], axis=0)
    norm_wait(0)


def orthonormal(*args):
    mom_sq, grad_sq, basis_sq, mom_nw, grad_nw, basis_nw = args
    rows = mom_sq.shape[1]
    wide, thin = mom_sq.shape[2], mom_nw.shape[2]
    widths = (wide // 2 + thin, wide // 2, wide // 2, wide // 2 + thin)
    vmem = pltpu.VMEM
    dma = pltpu.SemaphoreType.DMA
    whole = pl.BlockSpec(memory_space=pltpu.VMEM)
    return pl.pallas_call(
        orthonormal_kernel,
        out_shape=(
            pltpu.VMEM(mom_sq.shape, F32),
            pltpu.VMEM(mom_nw.shape, F32),
            pltpu.VMEM((4, rows, RANK), F32),
            pltpu.VMEM((2, RANK, wide), F32),
            pltpu.VMEM((2, RANK, thin), F32),
            pltpu.VMEM((8, RANK), F32),
        ),
        in_specs=[pl.BlockSpec(memory_space=pltpu.HBM)] * 6,
        out_specs=(whole,) * 6,
        scratch_shapes=[
            vmem(grad_sq.shape, BF16),
            vmem(basis_sq.shape, F32),
            vmem(grad_nw.shape, BF16),
            vmem(basis_nw.shape, F32),
            vmem(mom_sq.shape, BF16),
            vmem(mom_sq.shape, BF16),
            vmem(mom_nw.shape, BF16),
            vmem(mom_nw.shape, BF16),
            vmem((4, rows, RANK), F32),
            vmem((4, rows // 2, RANK), F32),
            vmem((4, rows, RANK), F32),
            vmem((2, 6, rows // 8, RANK), F32),
            vmem((128, RANK), F32),
            vmem((16, 8, RANK), F32),
            vmem((RANK, RANK), F32),
            vmem((RANK, 2 * RANK), F32),
            vmem((4, RANK, RANK), F32),
            vmem((RANK, rows), BF16),
            vmem((RANK, rows), BF16),
            *[vmem((RANK, w), F32) for w in widths],
            *[vmem((RANK, w), F32) for w in widths],
            *[vmem((6, 32, w), F32) for w in widths],
            *[vmem((3, 16, w), F32) for w in widths],
            vmem((8, 8, RANK), F32),
            vmem((288, RANK), F32),
            dma((9,)),
            dma((28,)),
            dma((111,)),
            dma((4,)),
            dma((2,)),
        ],
        compiler_params=pltpu.CompilerParams(
            collective_id=0, has_side_effects=True, vmem_limit_bytes=VMEM_LIMIT
        ),
        cost_estimate=pl.CostEstimate(flops=6 * 10**9, bytes_accessed=9 * 2**20, transcendentals=0),
        name="orthonormal",
    )(*(pltpu.with_memory_space_constraint(a, pltpu.HBM) for a in args))


def finish_kernel(
    scale_sq, scale_nw,
    buf_sq, buf_nw, left, back_sq, back_nw, squares,
    mom_sq_out, basis_sq_out, upd_sq_out, mom_nw_out, basis_nw_out, upd_nw_out,
    mom_sq, basis_sq, upd_sq, mom_nw, basis_nw, upd_nw, store_sem,
):
    rows = buf_sq.shape[1]
    pieces = 2
    piece = rows // pieces
    stores = []

    def store(src, dst):
        c = pltpu.make_async_copy(src, dst, store_sem.at[len(stores)])
        c.start()
        stores.append(c)

    def part(mom, upd, buf, factor, pair, divisor, scale):
        mom[...] = buf - mm((factor * (1.0 - MOMENTUM)).astype(BF16), pair[0])
        upd[...] = (scale * dot3(split(factor / divisor), pair)).astype(BF16)

    for k in range(2):
        divisor_sq, divisor_nw = (
            jnp.sqrt(squares[i : i + 1, :]) + 1e-06 for i in (k, 2 + k)
        )
        basis_sq[k] = back_sq[k].T / divisor_sq
        store(basis_sq.at[k], basis_sq_out.at[k])
        pair = split(back_sq[k])
        for p in range(pieces):
            r = pl.ds(p * piece, piece)
            part(mom_sq.at[k, r], upd_sq.at[k, r], buf_sq[k, r, :], left[k, r, :], pair, divisor_sq, scale_sq)
            store(mom_sq.at[k, r], mom_sq_out.at[k, r])
            store(upd_sq.at[k, r], upd_sq_out.at[k, r])
        basis_nw[k] = back_nw[k].T / divisor_nw
        part(mom_nw.at[k], upd_nw.at[k], buf_nw[k], left[2 + k], split(back_nw[k]), divisor_nw, scale_nw)
        store(mom_nw.at[k], mom_nw_out.at[k])
        store(basis_nw.at[k], basis_nw_out.at[k])
        store(upd_nw.at[k], upd_nw_out.at[k])
    for c in stores:
        c.wait()


def finish(buf_sq, buf_nw, left, back_sq, back_nw, squares, scale_sq, scale_nw):
    pairs, rows, wide = buf_sq.shape
    thin = buf_nw.shape[2]
    outs = (
        jax.ShapeDtypeStruct(buf_sq.shape, F32),
        jax.ShapeDtypeStruct((pairs, wide, RANK), F32),
        jax.ShapeDtypeStruct(buf_sq.shape, BF16),
        jax.ShapeDtypeStruct(buf_nw.shape, F32),
        jax.ShapeDtypeStruct((pairs, thin, RANK), F32),
        jax.ShapeDtypeStruct(buf_nw.shape, BF16),
    )

    def kernel(*refs):
        finish_kernel(scale_sq, scale_nw, *refs)

    return pl.pallas_call(
        kernel,
        out_shape=outs,
        in_specs=[pl.BlockSpec(memory_space=pltpu.VMEM)] * 6,
        out_specs=(pl.BlockSpec(memory_space=pltpu.HBM),) * 6,
        scratch_shapes=[pltpu.VMEM(o.shape, o.dtype) for o in outs]
        + [pltpu.SemaphoreType.DMA((16,))],
        compiler_params=pltpu.CompilerParams(vmem_limit_bytes=VMEM_LIMIT),
        cost_estimate=pl.CostEstimate(flops=3 * 10**9, bytes_accessed=9 * 2**20, transcendentals=0),
        name="finish",
    )(buf_sq, buf_nw, left, back_sq, back_nw, squares)


def local(momentum_square, grad_square, basis_square, momentum_narrow, grad_narrow, basis_narrow):
    parts = orthonormal(
        momentum_square, grad_square, basis_square, momentum_narrow, grad_narrow, basis_narrow
    )
    total_rows = momentum_square.shape[1] * lax.axis_size("fsdp")
    tp_count = lax.axis_size("tp")
    scale_sq = math.sqrt(total_rows * momentum_square.shape[2] * tp_count / RANK)
    scale_nw = math.sqrt(total_rows * momentum_narrow.shape[2] * tp_count / RANK)
    return finish(*parts, scale_sq, scale_nw)


def solution(mesh):
    by_both = P(None, "fsdp", "tp")
    by_tp = P(None, "tp", None)
    return jax.shard_map(
        local,
        mesh=mesh,
        in_specs=(by_both, by_both, by_tp, by_both, by_both, by_tp),
        out_specs=(by_both, by_tp, by_both, by_both, by_tp, by_both),
        check_vma=False,
    )
```

```python
import math

import jax
import jax.numpy as jnp
from jax import lax
from jax.experimental import pallas as pl
from jax.experimental.pallas import tpu as pltpu
from jax.sharding import PartitionSpec as P

RANK = 256
MOMENTUM = 0.9
MESH = pl.DeviceIdType.MESH
F32 = jnp.float32
BF16 = jnp.bfloat16
PANEL = 32
GROUP = 8
VMEM_LIMIT = 40 * 2**20

RING_X, RING_Y, RING_Z = 4, 4, 4


def split(x):
    hi = x.astype(BF16)
    return hi, (x - hi.astype(F32)).astype(BF16)


def mm(a, b, dims=((1,), (0,))):
    return lax.dot_general(a, b, (dims, ((), ())), preferred_element_type=F32)


def dot3(a, b, dims=((1,), (0,))):
    return mm(a[0], b[0], dims) + (mm(a[0], b[1], dims) + mm(a[1], b[0], dims))


def dot6(a, b, dims=((1,), (0,))):
    return lax.dot_general(
        a, b, (dims, ((), ())), precision=lax.Precision.HIGHEST, preferred_element_type=F32
    )


class Links:
    def __init__(self, send, recv):
        self.send, self.recv, self.sent, self.received = send, recv, 0, 0

    def group(self, ruler):
        return Group(self, ruler)


class Group:
    def __init__(self, links, ruler):
        self.links, self.ruler = links, ruler
        self.sem = links.send.at[links.sent]
        links.sent += 1

    def copy(self, src, dst, device):
        index = self.links.received
        self.links.received += 1
        return pltpu.make_async_remote_copy(
            src_ref=src,
            dst_ref=dst,
            send_sem=self.sem,
            recv_sem=self.links.recv.at[index],
            device_id=device,
            device_id_type=MESH,
        )

    def drain(self):
        pltpu.make_async_copy(self.ruler, self.ruler, self.sem).wait()


class Scatter:
    def __init__(self, links, me, right, left, part, half, inbox):
        self.me, self.part, self.half, self.inbox = me, part, half, inbox
        self.after, self.before = lax.rem(me + 1, 4), lax.rem(me + 3, 4)
        opposite = lax.rem(me + 2, 4)
        self.group = links.group(inbox)

        def outgoing(slot, view, device):
            return self.group.copy(view, inbox.at[slot], device)

        h = half
        self.r1 = outgoing(0, part(opposite, 0, h), right)
        self.r2 = outgoing(1, part(self.after, h, h), right)
        self.r3 = outgoing(2, part(self.after, 0, h), right)
        self.l1 = outgoing(3, part(opposite, h, h), left)
        self.l2 = outgoing(4, part(self.before, 0, h), left)
        self.l3 = outgoing(5, part(self.before, h, h), left)

    def start(self):
        self.r1.start()
        self.l1.start()

    def start_rest(self):
        self.r2.start()
        self.l2.start()

    def middle(self):
        h = self.half
        self.r1.wait_recv()
        view = self.part(self.after, 0, h)
        view[...] = view[...] + self.inbox[0]
        self.r3.start()
        self.l1.wait_recv()
        view = self.part(self.before, h, h)
        view[...] = view[...] + self.inbox[3]
        self.l3.start()

    def end(self, target):
        h = self.half
        self.r2.wait_recv()
        self.l2.wait_recv()
        self.r3.wait_recv()
        target(0, h)[...] = self.part(self.me, 0, h)[...] + (self.inbox[2] + self.inbox[4])
        self.l3.wait_recv()
        target(h, h)[...] = self.part(self.me, h, h)[...] + (self.inbox[1] + self.inbox[5])


class Gather:
    def __init__(self, links, me, right, left, part, half, ruler):
        after, before = lax.rem(me + 1, 4), lax.rem(me + 3, 4)
        self.group = links.group(ruler)
        h = half

        def outgoing(view, device):
            return self.group.copy(view, view, device)

        self.r1 = outgoing(part(me, 0, 2 * h), right)
        self.l1 = outgoing(part(me, 0, 2 * h), left)
        self.r2 = outgoing(part(before, 0, h), right)
        self.l2 = outgoing(part(after, h, h), left)

    def start(self):
        self.r1.start()
        self.l1.start()

    def middle(self):
        self.r1.wait_recv()
        self.r2.start()
        self.l1.wait_recv()
        self.l2.start()

    def end(self):
        self.r2.wait_recv()
        self.l2.wait_recv()


class DirectScatter:
    def __init__(self, links, me, device_of, part, rows, inbox):
        self.me, self.part, self.rows, self.inbox = me, part, rows, inbox
        self.group = links.group(inbox)
        self.copies = []
        for by in (2, 1, 3):
            peer = lax.rem(me + by, 4)
            view = part(peer, 0, rows)
            self.copies.append(self.group.copy(view, inbox.at[by - 1], device_of(peer)))

    def start(self):
        for c in self.copies:
            c.start()

    def end(self, target):
        for c in self.copies:
            c.wait_recv()
        own = self.part(self.me, 0, self.rows)[...]
        target(0, self.rows)[...] = (own + self.inbox[0]) + (self.inbox[1] + self.inbox[2])


class DirectGather:
    def __init__(self, links, me, device_of, part, rows, ruler):
        self.group = links.group(ruler)
        view = part(me, 0, rows)
        self.copies = [
            self.group.copy(view, view, device_of(lax.rem(me + by, 4))) for by in (2, 1, 3)
        ]

    def start(self):
        for c in self.copies:
            c.start()

    def end(self):
        for c in self.copies:
            c.wait_recv()


def factor_block(a):
    rows = lax.broadcasted_iota(jnp.int32, (PANEL, 128), 0)
    done = []
    for s in range(0, PANEL, GROUP):
        n = PANEL - s
        cols = [jnp.broadcast_to(a[s:, s + j : s + j + 1], (n, 128)) for j in range(GROUP)]
        lines = [a[s + j : s + j + 1, :] for j in range(GROUP)]
        rest = a[s + GROUP :]
        for j in range(GROUP):
            pivot = cols[j][j : j + 1, :]
            m = jnp.where(rows[s:] > s + j, cols[j] * (1.0 / pivot), 0.0)
            for q in range(j + 1, GROUP):
                cols[q] = cols[q] - m * cols[q][j : j + 1, :]
            for q in range(j + 1, GROUP):
                lines[q] = lines[q] - m[q : q + 1, :] * lines[j]
            if n > GROUP:
                rest = rest - m[GROUP:] * lines[j]
            done.append(lines[j] * lax.rsqrt(pivot))
        if n > GROUP:
            a = jnp.concatenate([a[: s + GROUP], rest], axis=0)
    return jnp.concatenate(done, axis=0)


def cholesky_start(gram, work):
    n = RANK
    work[:, :n] = gram[...]
    eye = lax.broadcasted_iota(jnp.int32, (n, n), 0) == lax.broadcasted_iota(jnp.int32, (n, n), 1)
    work[:, n:] = eye.astype(F32)


def cholesky_panels(work, inverse, first, last):
    n = RANK
    lane = lax.broadcasted_iota(jnp.int32, (PANEL, 128), 1)
    row = lax.broadcasted_iota(jnp.int32, (PANEL, 128), 0)

    def panel(k, carry):
        off = pl.multiple_of(k * PANEL, PANEL)
        band = work[pl.ds(off, PANEL), :]
        block = pltpu.roll(band[:, :n], lax.rem(n - off, n), axis=1)[:, :128]
        both = jnp.where(lane < PANEL, block, jnp.where(lane == row + PANEL, 1.0, 0.0))
        block_inverse = factor_block(both)[:, PANEL : 2 * PANEL]
        band = dot6(block_inverse, band)
        inverse[pl.ds(off, PANEL), :] = band[:, n:]
        work[...] = work[...] - dot6(band[:, :n], band, ((0,), (0,)))
        return carry

    lax.fori_loop(first, last, panel, 0)


def orthonormal_kernel(
    mom_sq, grad_sq, basis_sq, mom_nw, grad_nw, basis_nw,
    buf_sq, buf_nw, left_out, back_sq, back_nw, squares_out,
    grad_sq_v, basis_sq_v, grad_nw_v, basis_nw_v,
    sq_hi, sq_lo, nw_hi, nw_lo,
    partial, held, projected, scatter_z,
    gram_part, gram_in, gram, chol_work, inverse,
    turned_hi, turned_lo,
    sums_0, sums_1, sums_2, sums_3, wide_0, wide_1, wide_2, wide_3,
    scatter_0, scatter_1, scatter_2, scatter_3, scatter_4, scatter_5, scatter_6, scatter_7,
    norms, rulers,
    load_sem, send_sem, recv_sem, gram_sem, norm_sem,
):
    f, t = lax.axis_index("fsdp"), lax.axis_index("tp")
    y, x = f // RING_X, lax.rem(f, RING_X)
    z, core = t // 2, lax.rem(t, 2)
    other = 1 - core
    fsdp_count = RING_X * RING_Y
    tp_count = RING_Z * 2
    links = Links(send_sem, recv_sem)
    gram_ruler = gram_in.at[pl.ds(0, fsdp_count - 1)]

    def at(y=y, x=x, z=z, core=core):
        return (y * RING_X + x, z * 2 + core)

    def step(value, by):
        return lax.rem(value + by, 4)

    sibling = at(core=other)
    x_ring = (x, at(x=step(x, 1)), at(x=step(x, 3)))
    y_ring = (y, at(y=step(y, 1)), at(y=step(y, 3)))
    z_ring = (z, at(z=step(z, 1)), at(z=step(z, 3)))

    barrier = pltpu.get_barrier_semaphore()

    def greet_fsdp(k, carry):
        peer = lax.rem(f + k, fsdp_count)
        pl.semaphore_signal(barrier, inc=1, device_id=(peer, t), device_id_type=MESH)
        return carry

    def greet_tp(k, carry):
        peer = lax.rem(t + k, tp_count)
        pl.semaphore_signal(barrier, inc=1, device_id=(f, peer), device_id_type=MESH)
        return carry

    loads = []

    def load(src, dst):
        c = pltpu.make_async_copy(src, dst, load_sem.at[len(loads)])
        c.start()
        loads.append(c)

    load(basis_nw, basis_nw_v)
    load(mom_nw, buf_nw)
    load(grad_nw, grad_nw_v)
    for k in range(2):
        load(basis_sq.at[k], basis_sq_v.at[k])
        load(mom_sq.at[k], buf_sq.at[k])
        load(grad_sq.at[k], grad_sq_v.at[k])
    lax.fori_loop(1, fsdp_count, greet_fsdp, 0)
    lax.fori_loop(1, tp_count, greet_tp, 0)

    def rows_of(which):
        return pl.ds(pl.multiple_of(which * 256, 256), 256)

    core_group = links.group(held)
    core_copies = [
        core_group.copy(partial.at[i, rows_of(other)], held.at[i], sibling) for i in range(4)
    ]

    def project(i, buf, grad, basis, hi, lo, greeted=True):
        pair = split(basis[...])
        for place, which in enumerate((other, core)):
            rows = rows_of(which)
            b = buf[rows, :] + grad[rows, :].astype(F32)
            buf[rows, :] = b
            b_hi, b_lo = split(b)
            hi[rows, :] = b_hi
            lo[rows, :] = b_lo
            partial[i, rows, :] = dot3((b_hi, b_lo), pair)
            if place == 0:
                if not greeted:
                    pl.semaphore_wait(barrier, fsdp_count + tp_count - 2)
                core_copies[i].start()

    def own_rows(r, i, a, n):
        return projected.at[i, pl.ds(pl.multiple_of(core * 256 + r * 128 + a, 64), n)]

    def held_rows(r):
        return lambda i, a, n: held.at[i, pl.ds(r * 128 + a, n)]

    z_sum = [Scatter(links, *z_ring, held_rows(r), 64, scatter_z.at[r]) for r in range(2)]
    z_all = [
        Gather(links, *z_ring, lambda i, a, n, r=r: own_rows(r, i, a, n), 64, scatter_z.at[r])
        for r in range(2)
    ]
    across_groups = [links.group(partial.at[r]) for r in range(2)]

    def core_send(r, i):
        view = own_rows(r, i, 0, 128)
        return across_groups[r].copy(view, view, sibling)

    across = [[core_send(r, step(z, by)) for by in (0, 3, 1, 2)] for r in range(2)]

    def z_wait(r):
        for c in across[r][1:]:
            c.wait_recv()

    def z_turn(r):
        z_sum[r].end(lambda a, n: own_rows(r, z, a, n))
        z_all[r].start()
        across[r][0].start()

    def z_middle(r):
        z_all[r].middle()
        across[r][1].start()
        across[r][2].start()

    def z_end(r):
        z_all[r].end()
        across[r][3].start()

    for c in loads[:3]:
        c.wait()
    for k in range(2):
        project(
            2 + k, buf_nw.at[k], grad_nw_v.at[k], basis_nw_v.at[k], nw_hi.at[k], nw_lo.at[k], k > 0
        )
    for k in range(2):
        for c in loads[3 + k * 3 : 6 + k * 3]:
            c.wait()
        project(k, buf_sq.at[k], grad_sq_v.at[k], basis_sq_v.at[k], sq_hi.at[k], sq_lo.at[k])
    for i in (2, 3, 0, 1):
        core_copies[i].wait_recv()
        held[i] = held[i] + partial[i, rows_of(core), :]
    z_sum[0].start()
    z_sum[0].start_rest()
    z_sum[1].start()
    z_sum[0].middle()
    z_sum[1].start_rest()
    z_sum[1].middle()
    z_turn(0)
    z_turn(1)

    def gram_rows(i):
        return pl.ds(pl.multiple_of(i * 8, 8), 8)

    def gram_copy(peer, slot):
        return pltpu.make_async_remote_copy(
            src_ref=gram_part.at[gram_rows(peer)],
            dst_ref=gram_in.at[slot],
            send_sem=gram_sem.at[0],
            recv_sem=gram_sem.at[1],
            device_id=(peer, t),
            device_id_type=MESH,
        )

    def full_rows(i):
        return pl.ds(pl.multiple_of(core * 128 + i * 8, 8), 8)

    def gram_copy2(peer):
        view = gram.at[full_rows(f)]
        return pltpu.make_async_remote_copy(
            src_ref=view,
            dst_ref=view,
            send_sem=gram_sem.at[2],
            recv_sem=gram_sem.at[3],
            device_id=(peer, t),
            device_id_type=MESH,
        )

    def gram_wait(which):
        ruler = gram_ruler
        pltpu.make_async_copy(ruler, ruler, gram_sem.at[which]).wait()

    def gram_out(k, carry):
        gram_copy(lax.rem(f + k, fsdp_count), f).start()
        return carry

    def gram_out2(k, carry):
        gram_copy2(lax.rem(f + k, fsdp_count)).start()
        return carry

    sums = (sums_0, sums_1, sums_2, sums_3)
    wides = (wide_0, wide_1, wide_2, wide_3)
    inboxes = (scatter_0, scatter_1, scatter_2, scatter_3)
    inboxes_2 = (scatter_4, scatter_5, scatter_6, scatter_7)
    outer = (x_ring, y_ring, x_ring, y_ring)
    inner = (y_ring, x_ring, y_ring, x_ring)

    def thick(ref):
        return lambda i, a, n: ref.at[pl.ds(pl.multiple_of(i * 64 + a, 32), n)]

    def thin(ref, p):
        place = outer[p][0] * 64
        return lambda i, a, n: ref.at[pl.ds(pl.multiple_of(place + i * 16 + a, 16), n)]

    sum_1 = [Scatter(links, *outer[p], thick(sums[p]), 32, inboxes[p]) for p in range(4)]
    def on_x(i):
        return at(x=i)

    def on_y(i):
        return at(y=i)

    across_of = (on_y, on_x, on_y, on_x)
    sum_2 = [
        DirectScatter(links, inner[p][0], across_of[p], thin(sums[p], p), 16, inboxes_2[p])
        for p in range(4)
    ]
    all_1 = [
        DirectGather(links, inner[p][0], across_of[p], thin(wides[p], p), 16, inboxes_2[p])
        for p in range(4)
    ]
    all_2 = [Gather(links, *outer[p], thick(wides[p]), 32, inboxes[p]) for p in range(4)]

    def sum_1_end(p):
        sum_1[p].end(lambda a, n: thick(sums[p])(outer[p][0], a, n))
        sum_2[p].start()

    def sum_2_end(p):
        sum_2[p].end(lambda a, n: thin(wides[p], p)(inner[p][0], a, n))
        all_1[p].start()

    def all_1_end(p):
        all_1[p].end()
        all_2[p].start()

    half_cols = sq_hi.shape[2] // 2

    def narrow_back(k):
        factor = split(projected[2 + k].T)
        sums[3 * k][:, half_cols:] = dot3(factor, (nw_hi[k], nw_lo[k]))

    def square_back(k):
        turned_hi[...], turned_lo[...] = split(projected[k].T)
        for h in range(2):
            cols = slice(h * half_cols, (h + 1) * half_cols)
            part = dot3((turned_hi[...], turned_lo[...]), (sq_hi[k, :, cols], sq_lo[k, :, cols]))
            sums[2 * k + h][:, :half_cols] = part
            sum_1[2 * k + h].start()
            if k == 0:
                sum_1[h].start_rest()

    for r in range(2):
        across[r][0].wait_recv()
    gram_cols = pl.ds(pl.multiple_of(core * 128, 128), 128)
    gram_part[...] = dot6(projected[z, :, gram_cols], projected[z], ((0,), (0,)))
    lax.fori_loop(1, fsdp_count, gram_out, 0)
    z_middle(0)
    z_middle(1)
    gram_wait(1)
    gram_in[f] = gram_part[gram_rows(f), :]
    gram[full_rows(f), :] = jnp.sum(gram_in[...], axis=0)
    lax.fori_loop(1, fsdp_count, gram_out2, 0)
    z_end(0)
    z_end(1)
    z_wait(0)
    z_wait(1)
    narrow_back(0)
    square_back(0)
    narrow_back(1)
    square_back(1)
    gram_wait(3)
    half_rows = gram.at[pl.ds(pl.multiple_of(core * 128, 128), 128)]
    gram_across_group = links.group(half_rows)
    gram_across = gram_across_group.copy(half_rows, half_rows, sibling)
    gram_across.start()
    gram_across.wait_recv()

    own_inverse = inverse.at[z]
    cholesky_start(gram, chol_work)

    class Band:
        def __init__(self, first, rows):
            share = rows // 2

            def part(i, a, n):
                row = pl.multiple_of(first + core * share + a, 16)
                return inverse.at[i, pl.ds(row, n)]

            ruler = rulers.at[pl.ds(0, 3 * share)]
            self.ring = Gather(links, *z_ring, part, share // 2, ruler)
            self.group = links.group(ruler)
            views = [part(step(z, by), 0, share) for by in (3, 1, 2)]
            self.across = [self.group.copy(v, v, sibling) for v in views]

        def start(self):
            self.ring.start()

        def middle(self):
            self.ring.middle()
            self.across[0].start()
            self.across[1].start()

        def end(self):
            self.ring.end()
            self.across[2].start()

        def wait(self):
            for c in self.across:
                c.wait_recv()

    bands = [Band(0, 192), Band(192, 64)]

    def panels(first, last):
        cholesky_panels(chol_work, own_inverse, first, last)

    panels(0, 2)
    for p in (0, 1):
        sum_1[p].middle()
    for p in (2, 3):
        sum_1[p].start_rest()
    panels(2, 3)
    for p in (2, 3):
        sum_1[p].middle()
    panels(3, 5)
    for p in (0, 1):
        sum_1_end(p)
    panels(5, 6)
    for p in (2, 3):
        sum_1_end(p)
    for p in (0, 1):
        sum_2_end(p)
    panels(6, 7)
    for p in (2, 3):
        sum_2_end(p)
    panels(7, 8)
    bands[0].start()
    bands[1].start()
    for p in (0, 1):
        all_1_end(p)
    bands[0].middle()
    bands[1].middle()
    for p in (2, 3):
        all_1_end(p)
    for p in (0, 1):
        all_2[p].middle()
    bands[0].end()
    bands[1].end()
    for p in (2, 3):
        all_2[p].middle()
    bands[0].wait()
    bands[1].wait()

    norms[t] = jnp.zeros((8, RANK), F32)

    def back_factor(i, source, target):
        back = dot3(split(inverse[i]), split(source))
        target[...] = back
        square = jnp.sum(back * back, axis=1, keepdims=True)
        square = jnp.broadcast_to(square, (RANK, 128)).T
        norms[t, pl.ds(i, 1), :] = norms[t, pl.ds(i, 1), :] + square[:1]

    def back_factors(p):
        all_2[p].end()
        k, h = p // 2, p % 2
        cols = slice(h * half_cols, (h + 1) * half_cols)
        back_factor(k, wides[p][:, :half_cols], back_sq.at[k, :, cols])
        if k == h:
            back_factor(2 + k, wides[p][:, half_cols:], back_nw.at[k])

    def left_factor(i):
        left_out[i] = dot3(split(projected[i]), split(inverse[i]), ((1,), (1,)))

    for i in range(4):
        left_factor(i)
    back_factors(0)
    back_factors(1)
    back_factors(2)
    back_factors(3)

    def norm_copy(peer):
        return pltpu.make_async_remote_copy(
            src_ref=norms.at[t],
            dst_ref=norms.at[t],
            send_sem=norm_sem.at[0],
            recv_sem=norm_sem.at[1],
            device_id=(f, peer),
            device_id_type=MESH,
        )

    def norm_wait(which):
        ruler = norms.at[pl.ds(0, tp_count - 1)]
        pltpu.make_async_copy(ruler, ruler, norm_sem.at[which]).wait()

    def norm_out(k, carry):
        norm_copy(lax.rem(t + k, tp_count)).start()
        return carry

    lax.fori_loop(1, tp_count, norm_out, 0)

    for k in range(2):
        for buf, i, back in ((buf_sq, k, back_sq), (buf_nw, 2 + k, back_nw)):
            factor = (left_out[i] * (1.0 - MOMENTUM)).astype(BF16)
            buf[k] = buf[k] - mm(factor, back[k].astype(BF16))

    for group in [core_group, gram_across_group] + across_groups:
        group.drain()
    for band in bands:
        band.ring.group.drain()
        band.group.drain()
    for ring in z_sum + z_all + sum_1 + sum_2 + all_1 + all_2:
        ring.group.drain()
    gram_wait(0)
    gram_wait(2)
    norm_wait(1)
    squares_out[...] = jnp.sum(norms[...], axis=0)
    norm_wait(0)


def orthonormal(*args):
    mom_sq, grad_sq, basis_sq, mom_nw, grad_nw, basis_nw = args
    rows = mom_sq.shape[1]
    wide, thin = mom_sq.shape[2], mom_nw.shape[2]
    widths = (wide // 2 + thin, wide // 2, wide // 2, wide // 2 + thin)
    vmem = pltpu.VMEM
    dma = pltpu.SemaphoreType.DMA
    whole = pl.BlockSpec(memory_space=pltpu.VMEM)
    return pl.pallas_call(
        orthonormal_kernel,
        out_shape=(
            pltpu.VMEM(mom_sq.shape, F32),
            pltpu.VMEM(mom_nw.shape, F32),
            pltpu.VMEM((4, rows, RANK), F32),
            pltpu.VMEM((2, RANK, wide), F32),
            pltpu.VMEM((2, RANK, thin), F32),
            pltpu.VMEM((8, RANK), F32),
        ),
        in_specs=[pl.BlockSpec(memory_space=pltpu.HBM)] * 6,
        out_specs=(whole,) * 6,
        scratch_shapes=[
            vmem(grad_sq.shape, BF16),
            vmem(basis_sq.shape, F32),
            vmem(grad_nw.shape, BF16),
            vmem(basis_nw.shape, F32),
            vmem(mom_sq.shape, BF16),
            vmem(mom_sq.shape, BF16),
            vmem(mom_nw.shape, BF16),
            vmem(mom_nw.shape, BF16),
            vmem((4, rows, RANK), F32),
            vmem((4, rows // 2, RANK), F32),
            vmem((4, rows, RANK), F32),
            vmem((2, 6, rows // 8, RANK), F32),
            vmem((128, RANK), F32),
            vmem((16, 8, RANK), F32),
            vmem((RANK, RANK), F32),
            vmem((RANK, 2 * RANK), F32),
            vmem((4, RANK, RANK), F32),
            vmem((RANK, rows), BF16),
            vmem((RANK, rows), BF16),
            *[vmem((RANK, w), F32) for w in widths],
            *[vmem((RANK, w), F32) for w in widths],
            *[vmem((6, 32, w), F32) for w in widths],
            *[vmem((3, 16, w), F32) for w in widths],
            vmem((8, 8, RANK), F32),
            vmem((288, RANK), F32),
            dma((9,)),
            dma((28,)),
            dma((111,)),
            dma((4,)),
            dma((2,)),
        ],
        compiler_params=pltpu.CompilerParams(
            collective_id=0, has_side_effects=True, vmem_limit_bytes=VMEM_LIMIT
        ),
        cost_estimate=pl.CostEstimate(flops=6 * 10**9, bytes_accessed=9 * 2**20, transcendentals=0),
        name="orthonormal",
    )(*(pltpu.with_memory_space_constraint(a, pltpu.HBM) for a in args))


def finish_kernel(
    scale_sq, scale_nw,
    mom_sq, mom_nw, left, back_sq, back_nw, squares,
    mom_sq_out, basis_sq_out, upd_sq_out, mom_nw_out, basis_nw_out, upd_nw_out,
    basis_sq, upd_sq, basis_nw, upd_nw, store_sem,
):
    rows = upd_sq.shape[1]
    pieces = 2
    piece = rows // pieces
    stores = []

    def store(src, dst):
        c = pltpu.make_async_copy(src, dst, store_sem.at[len(stores)])
        c.start()
        stores.append(c)

    store(mom_sq, mom_sq_out)
    store(mom_nw, mom_nw_out)
    for k in range(2):
        divisor_sq, divisor_nw = (
            jnp.sqrt(squares[i : i + 1, :]) + 1e-06 for i in (k, 2 + k)
        )
        basis_sq[k] = back_sq[k].T / divisor_sq
        store(basis_sq.at[k], basis_sq_out.at[k])
        pair = split(back_sq[k])
        for p in range(pieces):
            r = pl.ds(p * piece, piece)
            factor = split(left[k, r, :] / divisor_sq)
            upd_sq[k, r, :] = (scale_sq * dot3(factor, pair)).astype(BF16)
            store(upd_sq.at[k, r], upd_sq_out.at[k, r])
        basis_nw[k] = back_nw[k].T / divisor_nw
        store(basis_nw.at[k], basis_nw_out.at[k])
        factor = split(left[2 + k] / divisor_nw)
        upd_nw[k] = (scale_nw * dot3(factor, split(back_nw[k]))).astype(BF16)
        store(upd_nw.at[k], upd_nw_out.at[k])
    for c in stores:
        c.wait()


def finish(mom_sq, mom_nw, left, back_sq, back_nw, squares, scale_sq, scale_nw):
    pairs, rows, wide = mom_sq.shape
    thin = mom_nw.shape[2]
    outs = (
        jax.ShapeDtypeStruct(mom_sq.shape, F32),
        jax.ShapeDtypeStruct((pairs, wide, RANK), F32),
        jax.ShapeDtypeStruct(mom_sq.shape, BF16),
        jax.ShapeDtypeStruct(mom_nw.shape, F32),
        jax.ShapeDtypeStruct((pairs, thin, RANK), F32),
        jax.ShapeDtypeStruct(mom_nw.shape, BF16),
    )

    def kernel(*refs):
        finish_kernel(scale_sq, scale_nw, *refs)

    return pl.pallas_call(
        kernel,
        out_shape=outs,
        in_specs=[pl.BlockSpec(memory_space=pltpu.VMEM)] * 6,
        out_specs=(pl.BlockSpec(memory_space=pltpu.HBM),) * 6,
        scratch_shapes=[pltpu.VMEM(outs[i].shape, outs[i].dtype) for i in (1, 2, 4, 5)]
        + [pltpu.SemaphoreType.DMA((12,))],
        compiler_params=pltpu.CompilerParams(vmem_limit_bytes=VMEM_LIMIT),
        cost_estimate=pl.CostEstimate(flops=2 * 10**9, bytes_accessed=9 * 2**20, transcendentals=0),
        name="finish",
    )(mom_sq, mom_nw, left, back_sq, back_nw, squares)


def local(momentum_square, grad_square, basis_square, momentum_narrow, grad_narrow, basis_narrow):
    parts = orthonormal(
        momentum_square, grad_square, basis_square, momentum_narrow, grad_narrow, basis_narrow
    )
    total_rows = momentum_square.shape[1] * lax.axis_size("fsdp")
    tp_count = lax.axis_size("tp")
    scale_sq = math.sqrt(total_rows * momentum_square.shape[2] * tp_count / RANK)
    scale_nw = math.sqrt(total_rows * momentum_narrow.shape[2] * tp_count / RANK)
    return finish(*parts, scale_sq, scale_nw)


def solution(mesh):
    by_both = P(None, "fsdp", "tp")
    by_tp = P(None, "tp", None)
    return jax.shard_map(
        local,
        mesh=mesh,
        in_specs=(by_both, by_both, by_tp, by_both, by_both, by_tp),
        out_specs=(by_both, by_tp, by_both, by_both, by_tp, by_both),
        check_vma=False,
    )
```

```python
import math

import jax
import jax.numpy as jnp
from jax import lax
from jax.experimental import pallas as pl
from jax.experimental.pallas import tpu as pltpu
from jax.sharding import PartitionSpec as P

RANK = 256
MOMENTUM = 0.9
MESH = pl.DeviceIdType.MESH
F32 = jnp.float32
BF16 = jnp.bfloat16
PANEL = 32
GROUP = 8
VMEM_LIMIT = 40 * 2**20

RING_X, RING_Y, RING_Z = 4, 4, 4


def split(x):
    hi = x.astype(BF16)
    return hi, (x - hi.astype(F32)).astype(BF16)


def mm(a, b, dims=((1,), (0,))):
    return lax.dot_general(a, b, (dims, ((), ())), preferred_element_type=F32)


def dot3(a, b, dims=((1,), (0,))):
    return mm(a[0], b[0], dims) + (mm(a[0], b[1], dims) + mm(a[1], b[0], dims))


def dot6(a, b, dims=((1,), (0,))):
    return lax.dot_general(
        a, b, (dims, ((), ())), precision=lax.Precision.HIGHEST, preferred_element_type=F32
    )


class Links:
    def __init__(self, send, recv):
        self.send, self.recv, self.sent, self.received = send, recv, 0, 0

    def group(self, ruler):
        return Group(self, ruler)


class Group:
    def __init__(self, links, ruler):
        self.links, self.ruler = links, ruler
        self.sem = links.send.at[links.sent]
        links.sent += 1

    def copy(self, src, dst, device):
        index = self.links.received
        self.links.received += 1
        return pltpu.make_async_remote_copy(
            src_ref=src,
            dst_ref=dst,
            send_sem=self.sem,
            recv_sem=self.links.recv.at[index],
            device_id=device,
            device_id_type=MESH,
        )

    def drain(self):
        pltpu.make_async_copy(self.ruler, self.ruler, self.sem).wait()


class Scatter:
    def __init__(self, links, me, right, left, part, half, inbox):
        self.me, self.part, self.half, self.inbox = me, part, half, inbox
        self.after, self.before = lax.rem(me + 1, 4), lax.rem(me + 3, 4)
        opposite = lax.rem(me + 2, 4)
        self.group = links.group(inbox)

        def outgoing(slot, view, device):
            return self.group.copy(view, inbox.at[slot], device)

        h = half
        self.r1 = outgoing(0, part(opposite, 0, h), right)
        self.r2 = outgoing(1, part(self.after, h, h), right)
        self.r3 = outgoing(2, part(self.after, 0, h), right)
        self.l1 = outgoing(3, part(opposite, h, h), left)
        self.l2 = outgoing(4, part(self.before, 0, h), left)
        self.l3 = outgoing(5, part(self.before, h, h), left)

    def start(self):
        self.r1.start()
        self.l1.start()

    def start_rest(self):
        self.r2.start()
        self.l2.start()

    def middle(self):
        h = self.half
        self.r1.wait_recv()
        view = self.part(self.after, 0, h)
        view[...] = view[...] + self.inbox[0]
        self.r3.start()
        self.l1.wait_recv()
        view = self.part(self.before, h, h)
        view[...] = view[...] + self.inbox[3]
        self.l3.start()

    def end(self, target):
        h = self.half
        self.r2.wait_recv()
        self.l2.wait_recv()
        self.r3.wait_recv()
        target(0, h)[...] = self.part(self.me, 0, h)[...] + (self.inbox[2] + self.inbox[4])
        self.l3.wait_recv()
        target(h, h)[...] = self.part(self.me, h, h)[...] + (self.inbox[1] + self.inbox[5])


class Gather:
    def __init__(self, links, me, right, left, part, half, ruler):
        after, before = lax.rem(me + 1, 4), lax.rem(me + 3, 4)
        self.group = links.group(ruler)
        h = half

        def outgoing(view, device):
            return self.group.copy(view, view, device)

        self.r1 = outgoing(part(me, 0, 2 * h), right)
        self.l1 = outgoing(part(me, 0, 2 * h), left)
        self.r2 = outgoing(part(before, 0, h), right)
        self.l2 = outgoing(part(after, h, h), left)

    def start(self):
        self.r1.start()
        self.l1.start()

    def middle(self):
        self.r1.wait_recv()
        self.r2.start()
        self.l1.wait_recv()
        self.l2.start()

    def end(self):
        self.r2.wait_recv()
        self.l2.wait_recv()


class DirectScatter:
    def __init__(self, links, me, device_of, part, rows, inbox):
        self.me, self.part, self.rows, self.inbox = me, part, rows, inbox
        self.group = links.group(inbox)
        self.copies = []
        for by in (2, 1, 3):
            peer = lax.rem(me + by, 4)
            view = part(peer, 0, rows)
            self.copies.append(self.group.copy(view, inbox.at[by - 1], device_of(peer)))

    def start(self):
        for c in self.copies:
            c.start()

    def end(self, target):
        for c in self.copies:
            c.wait_recv()
        own = self.part(self.me, 0, self.rows)[...]
        target(0, self.rows)[...] = (own + self.inbox[0]) + (self.inbox[1] + self.inbox[2])


class DirectGather:
    def __init__(self, links, me, device_of, part, rows, ruler):
        self.group = links.group(ruler)
        view = part(me, 0, rows)
        self.copies = [
            self.group.copy(view, view, device_of(lax.rem(me + by, 4))) for by in (2, 1, 3)
        ]

    def start(self):
        for c in self.copies:
            c.start()

    def end(self):
        for c in self.copies:
            c.wait_recv()


def factor_block(a):
    rows = lax.broadcasted_iota(jnp.int32, (PANEL, 128), 0)
    done = []
    for s in range(0, PANEL, GROUP):
        n = PANEL - s
        cols = [jnp.broadcast_to(a[s:, s + j : s + j + 1], (n, 128)) for j in range(GROUP)]
        lines = [a[s + j : s + j + 1, :] for j in range(GROUP)]
        rest = a[s + GROUP :]
        for j in range(GROUP):
            pivot = cols[j][j : j + 1, :]
            m = jnp.where(rows[s:] > s + j, cols[j] * (1.0 / pivot), 0.0)
            for q in range(j + 1, GROUP):
                cols[q] = cols[q] - m * cols[q][j : j + 1, :]
            for q in range(j + 1, GROUP):
                lines[q] = lines[q] - m[q : q + 1, :] * lines[j]
            if n > GROUP:
                rest = rest - m[GROUP:] * lines[j]
            done.append(lines[j] * lax.rsqrt(pivot))
        if n > GROUP:
            a = jnp.concatenate([a[: s + GROUP], rest], axis=0)
    return jnp.concatenate(done, axis=0)


def cholesky_start(gram, work):
    n = RANK
    work[:, :n] = gram[...]
    eye = lax.broadcasted_iota(jnp.int32, (n, n), 0) == lax.broadcasted_iota(jnp.int32, (n, n), 1)
    work[:, n:] = eye.astype(F32)


def cholesky_panels(work, inverse, first, last):
    n = RANK
    lane = lax.broadcasted_iota(jnp.int32, (PANEL, 128), 1)
    row = lax.broadcasted_iota(jnp.int32, (PANEL, 128), 0)

    def panel(k, carry):
        off = pl.multiple_of(k * PANEL, PANEL)
        band = work[pl.ds(off, PANEL), :]
        block = pltpu.roll(band[:, :n], lax.rem(n - off, n), axis=1)[:, :128]
        both = jnp.where(lane < PANEL, block, jnp.where(lane == row + PANEL, 1.0, 0.0))
        block_inverse = factor_block(both)[:, PANEL : 2 * PANEL]
        band = dot6(block_inverse, band)
        inverse[pl.ds(off, PANEL), :] = band[:, n:]
        work[...] = work[...] - dot6(band[:, :n], band, ((0,), (0,)))
        return carry

    lax.fori_loop(first, last, panel, 0)


def orthonormal_kernel(
    mom_sq, grad_sq, basis_sq, mom_nw, grad_nw, basis_nw,
    buf_sq, buf_nw, left_out, back_sq, back_nw, squares_out,
    grad_sq_v, basis_sq_v, grad_nw_v, basis_nw_v,
    sq_hi, sq_lo, nw_hi, nw_lo,
    partial, held, projected, scatter_z,
    gram_part, gram_in, gram, chol_work, inverse,
    turned_hi, turned_lo,
    sums_0, sums_1, sums_2, sums_3, wide_0, wide_1, wide_2, wide_3,
    scatter_0, scatter_1, scatter_2, scatter_3, scatter_4, scatter_5, scatter_6, scatter_7,
    norms, rulers,
    load_sem, send_sem, recv_sem, gram_sem, norm_sem,
):
    f, t = lax.axis_index("fsdp"), lax.axis_index("tp")
    y, x = f // RING_X, lax.rem(f, RING_X)
    z, core = t // 2, lax.rem(t, 2)
    other = 1 - core
    fsdp_count = RING_X * RING_Y
    tp_count = RING_Z * 2
    links = Links(send_sem, recv_sem)
    gram_ruler = gram_in.at[pl.ds(0, fsdp_count - 1)]

    def at(y=y, x=x, z=z, core=core):
        return (y * RING_X + x, z * 2 + core)

    def step(value, by):
        return lax.rem(value + by, 4)

    sibling = at(core=other)
    x_ring = (x, at(x=step(x, 1)), at(x=step(x, 3)))
    y_ring = (y, at(y=step(y, 1)), at(y=step(y, 3)))
    z_ring = (z, at(z=step(z, 1)), at(z=step(z, 3)))

    barrier = pltpu.get_barrier_semaphore()

    def greet_fsdp(k, carry):
        peer = lax.rem(f + k, fsdp_count)
        pl.semaphore_signal(barrier, inc=1, device_id=(peer, t), device_id_type=MESH)
        return carry

    def greet_tp(k, carry):
        peer = lax.rem(t + k, tp_count)
        pl.semaphore_signal(barrier, inc=1, device_id=(f, peer), device_id_type=MESH)
        return carry

    loads = []

    def load(src, dst):
        c = pltpu.make_async_copy(src, dst, load_sem.at[len(loads)])
        c.start()
        loads.append(c)

    load(basis_nw, basis_nw_v)
    load(mom_nw, buf_nw)
    load(grad_nw, grad_nw_v)
    for k in range(2):
        load(basis_sq.at[k], basis_sq_v.at[k])
        load(mom_sq.at[k], buf_sq.at[k])
        load(grad_sq.at[k], grad_sq_v.at[k])
    lax.fori_loop(1, fsdp_count, greet_fsdp, 0)
    lax.fori_loop(1, tp_count, greet_tp, 0)

    def rows_of(which):
        return pl.ds(pl.multiple_of(which * 256, 256), 256)

    core_group = links.group(held)
    core_copies = [
        core_group.copy(partial.at[i, rows_of(other)], held.at[i], sibling) for i in range(4)
    ]

    def project(i, buf, grad, basis, hi, lo, greeted=True):
        pair = split(basis[...])
        for place, which in enumerate((other, core)):
            rows = rows_of(which)
            b = buf[rows, :] + grad[rows, :].astype(F32)
            buf[rows, :] = b
            b_hi, b_lo = split(b)
            hi[rows, :] = b_hi
            lo[rows, :] = b_lo
            partial[i, rows, :] = dot3((b_hi, b_lo), pair)
            if place == 0:
                if not greeted:
                    pl.semaphore_wait(barrier, fsdp_count + tp_count - 2)
                core_copies[i].start()

    def own_rows(r, i, a, n):
        return projected.at[i, pl.ds(pl.multiple_of(core * 256 + r * 128 + a, 64), n)]

    def held_rows(r):
        return lambda i, a, n: held.at[i, pl.ds(r * 128 + a, n)]

    z_sum = [Scatter(links, *z_ring, held_rows(r), 64, scatter_z.at[r]) for r in range(2)]
    z_all = [
        Gather(links, *z_ring, lambda i, a, n, r=r: own_rows(r, i, a, n), 64, scatter_z.at[r])
        for r in range(2)
    ]
    across_groups = [links.group(partial.at[r]) for r in range(2)]

    def core_send(r, i):
        view = own_rows(r, i, 0, 128)
        return across_groups[r].copy(view, view, sibling)

    across = [[core_send(r, step(z, by)) for by in (0, 3, 1, 2)] for r in range(2)]

    def z_wait(r):
        for c in across[r][1:]:
            c.wait_recv()

    def z_turn(r):
        z_sum[r].end(lambda a, n: own_rows(r, z, a, n))
        z_all[r].start()
        across[r][0].start()

    def z_middle(r):
        z_all[r].middle()
        across[r][1].start()
        across[r][2].start()

    def z_end(r):
        z_all[r].end()
        across[r][3].start()

    for c in loads[:3]:
        c.wait()
    for k in range(2):
        project(
            2 + k, buf_nw.at[k], grad_nw_v.at[k], basis_nw_v.at[k], nw_hi.at[k], nw_lo.at[k], k > 0
        )
    for k in range(2):
        for c in loads[3 + k * 3 : 6 + k * 3]:
            c.wait()
        project(k, buf_sq.at[k], grad_sq_v.at[k], basis_sq_v.at[k], sq_hi.at[k], sq_lo.at[k])
    for i in (2, 3, 0, 1):
        core_copies[i].wait_recv()
        held[i] = held[i] + partial[i, rows_of(core), :]
    z_sum[0].start()
    z_sum[0].start_rest()
    z_sum[1].start()
    z_sum[0].middle()
    z_sum[1].start_rest()
    z_sum[1].middle()
    z_turn(0)
    z_turn(1)

    def gram_rows(i):
        return pl.ds(pl.multiple_of(i * 8, 8), 8)

    def gram_copy(peer, slot):
        return pltpu.make_async_remote_copy(
            src_ref=gram_part.at[gram_rows(peer)],
            dst_ref=gram_in.at[slot],
            send_sem=gram_sem.at[0],
            recv_sem=gram_sem.at[1],
            device_id=(peer, t),
            device_id_type=MESH,
        )

    def full_rows(i):
        return pl.ds(pl.multiple_of(core * 128 + i * 8, 8), 8)

    def gram_copy2(peer):
        view = gram.at[full_rows(f)]
        return pltpu.make_async_remote_copy(
            src_ref=view,
            dst_ref=view,
            send_sem=gram_sem.at[2],
            recv_sem=gram_sem.at[3],
            device_id=(peer, t),
            device_id_type=MESH,
        )

    def gram_wait(which):
        ruler = gram_ruler
        pltpu.make_async_copy(ruler, ruler, gram_sem.at[which]).wait()

    def gram_out(k, carry):
        gram_copy(lax.rem(f + k, fsdp_count), f).start()
        return carry

    def gram_out2(k, carry):
        gram_copy2(lax.rem(f + k, fsdp_count)).start()
        return carry

    sums = (sums_0, sums_1, sums_2, sums_3)
    wides = (wide_0, wide_1, wide_2, wide_3)
    inboxes = (scatter_0, scatter_1, scatter_2, scatter_3)
    inboxes_2 = (scatter_4, scatter_5, scatter_6, scatter_7)
    outer = (x_ring, y_ring, x_ring, y_ring)
    inner = (y_ring, x_ring, y_ring, x_ring)

    def thick(ref):
        return lambda i, a, n: ref.at[pl.ds(pl.multiple_of(i * 64 + a, 32), n)]

    def thin(ref, p):
        place = outer[p][0] * 64
        return lambda i, a, n: ref.at[pl.ds(pl.multiple_of(place + i * 16 + a, 16), n)]

    sum_1 = [Scatter(links, *outer[p], thick(sums[p]), 32, inboxes[p]) for p in range(4)]
    def on_x(i):
        return at(x=i)

    def on_y(i):
        return at(y=i)

    across_of = (on_y, on_x, on_y, on_x)
    sum_2 = [
        DirectScatter(links, inner[p][0], across_of[p], thin(sums[p], p), 16, inboxes_2[p])
        for p in range(4)
    ]
    all_1 = [
        DirectGather(links, inner[p][0], across_of[p], thin(wides[p], p), 16, inboxes_2[p])
        for p in range(4)
    ]
    all_2 = [Gather(links, *outer[p], thick(wides[p]), 32, inboxes[p]) for p in range(4)]

    def sum_1_end(p):
        sum_1[p].end(lambda a, n: thick(sums[p])(outer[p][0], a, n))
        sum_2[p].start()

    def sum_2_end(p):
        sum_2[p].end(lambda a, n: thin(wides[p], p)(inner[p][0], a, n))
        all_1[p].start()

    def all_1_end(p):
        all_1[p].end()
        all_2[p].start()

    half_cols = sq_hi.shape[2] // 2

    def narrow_back(k):
        factor = split(projected[2 + k].T)
        sums[3 * k][:, half_cols:] = dot3(factor, (nw_hi[k], nw_lo[k]))

    def square_back(k):
        turned_hi[...], turned_lo[...] = split(projected[k].T)
        for h in range(2):
            cols = slice(h * half_cols, (h + 1) * half_cols)
            part = dot3((turned_hi[...], turned_lo[...]), (sq_hi[k, :, cols], sq_lo[k, :, cols]))
            sums[2 * k + h][:, :half_cols] = part
            sum_1[2 * k + h].start()
            if k == 0:
                sum_1[h].start_rest()

    for r in range(2):
        across[r][0].wait_recv()
    gram_cols = pl.ds(pl.multiple_of(core * 128, 128), 128)
    gram_part[...] = dot6(projected[z, :, gram_cols], projected[z], ((0,), (0,)))
    lax.fori_loop(1, fsdp_count, gram_out, 0)
    z_middle(0)
    z_middle(1)
    gram_wait(1)
    gram_in[f] = gram_part[gram_rows(f), :]
    gram[full_rows(f), :] = jnp.sum(gram_in[...], axis=0)
    lax.fori_loop(1, fsdp_count, gram_out2, 0)
    z_end(0)
    z_end(1)
    z_wait(0)
    z_wait(1)
    narrow_back(0)
    square_back(0)
    narrow_back(1)
    square_back(1)
    gram_wait(3)
    half_rows = gram.at[pl.ds(pl.multiple_of(core * 128, 128), 128)]
    gram_across_group = links.group(half_rows)
    gram_across = gram_across_group.copy(half_rows, half_rows, sibling)
    gram_across.start()
    gram_across.wait_recv()

    own_inverse = inverse.at[z]
    cholesky_start(gram, chol_work)

    class Band:
        def __init__(self, first, rows):
            share = rows // 2

            def part(i, a, n):
                row = pl.multiple_of(first + core * share + a, 16)
                return inverse.at[i, pl.ds(row, n)]

            ruler = rulers.at[pl.ds(0, 3 * share)]
            self.ring = Gather(links, *z_ring, part, share // 2, ruler)
            self.group = links.group(ruler)
            views = [part(step(z, by), 0, share) for by in (3, 1, 2)]
            self.across = [self.group.copy(v, v, sibling) for v in views]

        def start(self):
            self.ring.start()

        def middle(self):
            self.ring.middle()
            self.across[0].start()
            self.across[1].start()

        def end(self):
            self.ring.end()
            self.across[2].start()

        def wait(self):
            for c in self.across:
                c.wait_recv()

    bands = [Band(0, 192), Band(192, 64)]

    def panels(first, last):
        cholesky_panels(chol_work, own_inverse, first, last)

    panels(0, 2)
    for p in (0, 1):
        sum_1[p].middle()
    for p in (2, 3):
        sum_1[p].start_rest()
    panels(2, 3)
    for p in (2, 3):
        sum_1[p].middle()
    panels(3, 5)
    for p in (0, 1):
        sum_1_end(p)
    panels(5, 6)
    bands[0].start()
    for p in (2, 3):
        sum_1_end(p)
    for p in (0, 1):
        sum_2_end(p)
    panels(6, 7)
    for p in (2, 3):
        sum_2_end(p)
    panels(7, 8)
    bands[1].start()
    for p in (0, 1):
        all_1_end(p)
    for p in (2, 3):
        all_1_end(p)
    bands[0].middle()
    bands[1].middle()
    for p in (0, 1):
        all_2[p].middle()
    for p in (2, 3):
        all_2[p].middle()
    bands[0].end()
    bands[1].end()
    bands[0].wait()
    bands[1].wait()

    norms[t] = jnp.zeros((8, RANK), F32)

    def back_factor(i, source, target):
        back = dot3(split(inverse[i]), split(source))
        target[...] = back
        square = jnp.sum(back * back, axis=1, keepdims=True)
        square = jnp.broadcast_to(square, (RANK, 128)).T
        norms[t, pl.ds(i, 1), :] = norms[t, pl.ds(i, 1), :] + square[:1]

    def back_factors(p):
        all_2[p].end()
        k, h = p // 2, p % 2
        cols = slice(h * half_cols, (h + 1) * half_cols)
        back_factor(k, wides[p][:, :half_cols], back_sq.at[k, :, cols])
        if k == h:
            back_factor(2 + k, wides[p][:, half_cols:], back_nw.at[k])

    def left_factor(i):
        left_out[i] = dot3(split(projected[i]), split(inverse[i]), ((1,), (1,)))

    for i in range(4):
        left_factor(i)
    back_factors(0)
    back_factors(1)
    back_factors(2)
    back_factors(3)

    def norm_copy(peer):
        return pltpu.make_async_remote_copy(
            src_ref=norms.at[t],
            dst_ref=norms.at[t],
            send_sem=norm_sem.at[0],
            recv_sem=norm_sem.at[1],
            device_id=(f, peer),
            device_id_type=MESH,
        )

    def norm_wait(which):
        ruler = norms.at[pl.ds(0, tp_count - 1)]
        pltpu.make_async_copy(ruler, ruler, norm_sem.at[which]).wait()

    def norm_out(k, carry):
        norm_copy(lax.rem(t + k, tp_count)).start()
        return carry

    lax.fori_loop(1, tp_count, norm_out, 0)

    for k in range(2):
        for buf, i, back in ((buf_sq, k, back_sq), (buf_nw, 2 + k, back_nw)):
            factor = (left_out[i] * (1.0 - MOMENTUM)).astype(BF16)
            buf[k] = buf[k] - mm(factor, back[k].astype(BF16))

    for group in [core_group, gram_across_group] + across_groups:
        group.drain()
    for band in bands:
        band.ring.group.drain()
        band.group.drain()
    for ring in z_sum + z_all + sum_1 + sum_2 + all_1 + all_2:
        ring.group.drain()
    gram_wait(0)
    gram_wait(2)
    norm_wait(1)
    squares_out[...] = jnp.sum(norms[...], axis=0)
    norm_wait(0)


def orthonormal(*args):
    mom_sq, grad_sq, basis_sq, mom_nw, grad_nw, basis_nw = args
    rows = mom_sq.shape[1]
    wide, thin = mom_sq.shape[2], mom_nw.shape[2]
    widths = (wide // 2 + thin, wide // 2, wide // 2, wide // 2 + thin)
    vmem = pltpu.VMEM
    dma = pltpu.SemaphoreType.DMA
    whole = pl.BlockSpec(memory_space=pltpu.VMEM)
    return pl.pallas_call(
        orthonormal_kernel,
        out_shape=(
            pltpu.VMEM(mom_sq.shape, F32),
            pltpu.VMEM(mom_nw.shape, F32),
            pltpu.VMEM((4, rows, RANK), F32),
            pltpu.VMEM((2, RANK, wide), F32),
            pltpu.VMEM((2, RANK, thin), F32),
            pltpu.VMEM((8, RANK), F32),
        ),
        in_specs=[pl.BlockSpec(memory_space=pltpu.HBM)] * 6,
        out_specs=(whole,) * 6,
        scratch_shapes=[
            vmem(grad_sq.shape, BF16),
            vmem(basis_sq.shape, F32),
            vmem(grad_nw.shape, BF16),
            vmem(basis_nw.shape, F32),
            vmem(mom_sq.shape, BF16),
            vmem(mom_sq.shape, BF16),
            vmem(mom_nw.shape, BF16),
            vmem(mom_nw.shape, BF16),
            vmem((4, rows, RANK), F32),
            vmem((4, rows // 2, RANK), F32),
            vmem((4, rows, RANK), F32),
            vmem((2, 6, rows // 8, RANK), F32),
            vmem((128, RANK), F32),
            vmem((16, 8, RANK), F32),
            vmem((RANK, RANK), F32),
            vmem((RANK, 2 * RANK), F32),
            vmem((4, RANK, RANK), F32),
            vmem((RANK, rows), BF16),
            vmem((RANK, rows), BF16),
            *[vmem((RANK, w), F32) for w in widths],
            *[vmem((RANK, w), F32) for w in widths],
            *[vmem((6, 32, w), F32) for w in widths],
            *[vmem((3, 16, w), F32) for w in widths],
            vmem((8, 8, RANK), F32),
            vmem((288, RANK), F32),
            dma((9,)),
            dma((28,)),
            dma((111,)),
            dma((4,)),
            dma((2,)),
        ],
        compiler_params=pltpu.CompilerParams(
            collective_id=0, has_side_effects=True, vmem_limit_bytes=VMEM_LIMIT
        ),
        cost_estimate=pl.CostEstimate(flops=6 * 10**9, bytes_accessed=9 * 2**20, transcendentals=0),
        name="orthonormal",
    )(*(pltpu.with_memory_space_constraint(a, pltpu.HBM) for a in args))


def finish_kernel(
    scale_sq, scale_nw,
    mom_sq, mom_nw, left, back_sq, back_nw, squares,
    mom_sq_out, basis_sq_out, upd_sq_out, mom_nw_out, basis_nw_out, upd_nw_out,
    basis_sq, upd_sq, basis_nw, upd_nw, store_sem,
):
    rows = upd_sq.shape[1]
    pieces = 2
    piece = rows // pieces
    stores = []

    def store(src, dst):
        c = pltpu.make_async_copy(src, dst, store_sem.at[len(stores)])
        c.start()
        stores.append(c)

    store(mom_sq, mom_sq_out)
    store(mom_nw, mom_nw_out)
    for k in range(2):
        divisor_sq, divisor_nw = (
            jnp.sqrt(squares[i : i + 1, :]) + 1e-06 for i in (k, 2 + k)
        )
        basis_sq[k] = back_sq[k].T / divisor_sq
        store(basis_sq.at[k], basis_sq_out.at[k])
        pair = split(back_sq[k])
        for p in range(pieces):
            r = pl.ds(p * piece, piece)
            factor = split(left[k, r, :] / divisor_sq)
            upd_sq[k, r, :] = (scale_sq * dot3(factor, pair)).astype(BF16)
            store(upd_sq.at[k, r], upd_sq_out.at[k, r])
        basis_nw[k] = back_nw[k].T / divisor_nw
        store(basis_nw.at[k], basis_nw_out.at[k])
        factor = split(left[2 + k] / divisor_nw)
        upd_nw[k] = (scale_nw * dot3(factor, split(back_nw[k]))).astype(BF16)
        store(upd_nw.at[k], upd_nw_out.at[k])
    for c in stores:
        c.wait()


def finish(mom_sq, mom_nw, left, back_sq, back_nw, squares, scale_sq, scale_nw):
    pairs, rows, wide = mom_sq.shape
    thin = mom_nw.shape[2]
    outs = (
        jax.ShapeDtypeStruct(mom_sq.shape, F32),
        jax.ShapeDtypeStruct((pairs, wide, RANK), F32),
        jax.ShapeDtypeStruct(mom_sq.shape, BF16),
        jax.ShapeDtypeStruct(mom_nw.shape, F32),
        jax.ShapeDtypeStruct((pairs, thin, RANK), F32),
        jax.ShapeDtypeStruct(mom_nw.shape, BF16),
    )

    def kernel(*refs):
        finish_kernel(scale_sq, scale_nw, *refs)

    return pl.pallas_call(
        kernel,
        out_shape=outs,
        in_specs=[pl.BlockSpec(memory_space=pltpu.VMEM)] * 6,
        out_specs=(pl.BlockSpec(memory_space=pltpu.HBM),) * 6,
        scratch_shapes=[pltpu.VMEM(outs[i].shape, outs[i].dtype) for i in (1, 2, 4, 5)]
        + [pltpu.SemaphoreType.DMA((12,))],
        compiler_params=pltpu.CompilerParams(vmem_limit_bytes=VMEM_LIMIT),
        cost_estimate=pl.CostEstimate(flops=2 * 10**9, bytes_accessed=9 * 2**20, transcendentals=0),
        name="finish",
    )(mom_sq, mom_nw, left, back_sq, back_nw, squares)


def local(momentum_square, grad_square, basis_square, momentum_narrow, grad_narrow, basis_narrow):
    parts = orthonormal(
        momentum_square, grad_square, basis_square, momentum_narrow, grad_narrow, basis_narrow
    )
    total_rows = momentum_square.shape[1] * lax.axis_size("fsdp")
    tp_count = lax.axis_size("tp")
    scale_sq = math.sqrt(total_rows * momentum_square.shape[2] * tp_count / RANK)
    scale_nw = math.sqrt(total_rows * momentum_narrow.shape[2] * tp_count / RANK)
    return finish(*parts, scale_sq, scale_nw)


def solution(mesh):
    by_both = P(None, "fsdp", "tp")
    by_tp = P(None, "tp", None)
    return jax.shard_map(
        local,
        mesh=mesh,
        in_specs=(by_both, by_both, by_tp, by_both, by_both, by_tp),
        out_specs=(by_both, by_tp, by_both, by_both, by_tp, by_both),
        check_vma=False,
    )
```
